32 devices in a mesh: tiles: 8 (over z, x), views: 4 (over y, core).
Axes of the slice: x: 2, y: 2, z: 4, core: 2. Of those that a mesh axis runs over, the one named last changes fastest.
Arguments:
- ref_features: bfloat16 [8, 8, 4096], P('tiles'), may hold values from -6 to 6
- partner_lines: bfloat16 [8, 4, 8, 8192], P('tiles'), may hold values from -6 to 6
- line_owner: int32 [8, 32, 1], P('tiles'), may hold values from 0 to 7; in each aligned block of 32 rows (0 to 31, 32 to 63, ..., all dimensions but the last counted through in order) at most 8 rows name the same one
- line_index: int32 [8, 32], P('tiles'), may hold values from 0 to 7
- line_offset: int32 [8, 32], P('tiles'), may hold values from 0 to 64
- neighbours: int32 [8, 4], replicated, may hold values from -1 to 7, as said below
- conv1_weight: bfloat16 [3, 3, 3, 8, 32], replicated, may hold values from -0.4375 to 0.4375
- conv1_bias: float32 [32], replicated, may hold values from -3 to 3
- conv2_weight: bfloat16 [3, 3, 3, 32, 32], replicated, may hold values from -0.21875 to 0.21875
- conv2_bias: float32 [32], replicated, may hold values from -3 to 3
Outputs:
- regularized: float32 [8, 64, 8, 4096], P('tiles', 'views')
The draws below stay inside these ranges and needn't reach their ends.
Inputs may be any that keep to these rules, and one draw needn't show every extreme that they name: `line_owner`: among the 32 requests of one tile (aligned blocks of rows), no owner is named more than 8 times. Tile positions in a grid of 2 rows and 4 columns are a permutation of the tiles; neighbours lists the tiles above, below, left and right, -1 at the grid's edge.
All inputs are finite; a program needn't handle non-finite values.
Results may differ from the reference program's by a relative error of at most 0.0019.
Values may be sent and summed in bfloat16 or wider, within the bound.
A program may use at most 128 MiB of HBM per device.

```python
import math
import jax
import jax.numpy as jnp
import numpy as np
from jax import lax

C = 32
G = 8
CH = 32
NDISP = 64
W = 128
SW = 256
NPV = 4
H = 8
MCOLS = 4
TILES = 8
NREQ = 32
CAP = 8


def draw_neighbours(key, part):
    placed = jax.random.permutation(key, TILES).astype(jnp.int32)
    positions = jnp.arange(TILES, dtype=jnp.int32)
    grid_row = positions // MCOLS
    grid_col = positions % MCOLS
    grid_height = TILES // MCOLS

    def tile_at(row_at, col_at, inside):
        spot = jnp.clip(row_at, 0, grid_height - 1) * MCOLS + jnp.clip(col_at, 0, MCOLS - 1)
        return jnp.where(inside, placed[spot], -1)
    links = jnp.stack([tile_at(grid_row - 1, grid_col, grid_row > 0), tile_at(grid_row + 1, grid_col, grid_row < grid_height - 1), tile_at(grid_row, grid_col - 1, grid_col > 0), tile_at(grid_row, grid_col + 1, grid_col < MCOLS - 1)], axis=1).astype(jnp.int32)
    return jnp.zeros((TILES, 4), jnp.int32).at[placed].set(links)


def set_ends(drawn, key, low, high):
    extent = drawn.shape
    spot = [jax.random.randint(jax.random.fold_in(key, axis), (), 0, extent[axis]) for axis in range(len(extent))]
    drawn = drawn.at[tuple(spot)].set(low)
    longest = extent.index(max(extent))
    spot[longest] = (spot[longest] + 1) % extent[longest]
    return drawn.at[tuple(spot)].set(high)


def level_of(own_key, dims, pieces, smallest, top_value):
    level, own = 1.0, jax.random.fold_in(own_key, 6)
    for position, parts in pieces:
        heights = jnp.exp(jax.random.uniform(jax.random.fold_in(own, position), (parts,), jnp.float32, smallest / len(pieces), top_value / len(pieces)))
        level = level * jnp.repeat(heights, dims[position] // parts).reshape([-1 if axis == position else 1 for axis in range(len(dims))])
    return level


def deal_out(stream_key, own, number, rows, count, top, limit, slope):
    sequence = jax.random.permutation(stream_key, count)
    heavy_load, usual = load_shares(count, rows * top, limit, slope, True), load_shares(count, rows * top, limit, slope, False)
    places = jnp.arange(count)

    def named(sizes, rotation):
        used = int((sizes > 0).sum())
        fixed = max(1, used // 4)
        moved = fixed + (places - fixed + rotation * (used - fixed)) % max(1, count - fixed)
        return jnp.zeros((count,), jnp.int32).at[sequence[jnp.where(places < fixed, places, moved)]].set(jnp.asarray(sizes, jnp.int32))

    sizes = jnp.where(number % 4 == 0, named(heavy_load, number // 4), named(usual, number - number // 4 - 1))
    mixed = jax.random.permutation(jax.random.fold_in(own, 3), count)
    giver, taker = mixed[0:count // 2 * 2:2], mixed[1:count // 2 * 2:2]
    room = jnp.minimum(sizes[giver] - 1, limit - sizes[taker]) // 2
    room = jnp.where((giver == sequence[0]) | (taker == sequence[0]) | (sizes[taker] == 0), 0, jnp.maximum(room, 0))
    moved = jax.random.randint(jax.random.fold_in(own, 4), (count // 2,), 0, 1 << 20) % (room + 1)
    sizes = sizes.at[giver].add(-moved).at[taker].add(moved)
    labels = jnp.searchsorted(jnp.cumsum(sizes), jnp.arange(rows * top), side="right").astype(jnp.int32)
    grid = labels.reshape(top, rows).T
    grid = grid[jax.random.permutation(jax.random.fold_in(own, 1), rows)]
    rotation = jax.random.randint(jax.random.fold_in(own, 2), (rows, 1), 0, top)
    return jnp.take_along_axis(grid, (jnp.arange(top)[None, :] + rotation) % top, axis=1)


def load_shares(count, total, limit, lean, full):
    portions = [(1 << 20) // math.isqrt(grade ** lean) + 1 for grade in range(1, count + 1)]
    largest = limit if full else min(limit, max(-(-total // count), total * portions[0] // sum(portions)))
    least = 1 if total - largest >= count - 1 else 0
    holding, rest = [largest] + [least] * (count - 1), total - largest - least * (count - 1)
    while rest > 0:
        candidates = [i for i in range(1, count) if holding[i] < largest] or [i for i in range(1, count) if holding[i] < limit]
        mass, budget = sum([portions[i] for i in candidates]), rest
        for i in candidates:
            more = min(limit - holding[i], max(1, budget * portions[i] // mass), rest)
            holding[i] = holding[i] + more
            rest = rest - more
    return np.array(holding)


def scatter_about(key, extent, width, limit, cuts=(), held_as=jnp.bfloat16):
    factor_of = level_of(key, extent, cuts, -0.22, 0.18) if cuts else 1.0
    entries = jax.random.normal(key, extent, jnp.float32) * width * factor_of
    return jnp.minimum(jnp.maximum(entries, -limit), limit).astype(held_as)


def setup_inputs(seed: int = 0) -> dict:
    key_of = jax.random.split(jax.random.key(seed), 11)
    ref_features = scatter_about(key_of[0], (TILES, H, W * C), 1.0, 6.0, ((0, 8),))
    partner_lines = scatter_about(key_of[1], (TILES, NPV, H, SW * C), 1.0, 6.0, ((0, 8),))
    line_owner_keys = jax.random.split(jax.random.fold_in(key_of[2], 1), TILES * NREQ // NREQ)
    line_owner_turns = jax.random.permutation(jax.random.fold_in(key_of[2], 3), TILES * NREQ // NREQ)
    line_owner = jax.vmap(lambda own, number: deal_out(jax.random.fold_in(key_of[2], 2), own, number, NREQ, TILES, 1, CAP, 2))(line_owner_keys, line_owner_turns).reshape((TILES, NREQ, 1))
    line_index = set_ends(jax.random.randint(key_of[3], (TILES, NREQ), 0, H), jax.random.fold_in(key_of[3], 1), 0, H - 1).astype(jnp.int32)
    line_offset = set_ends(jax.random.randint(key_of[4], (TILES, NREQ), 0, SW - W - NDISP + 1), jax.random.fold_in(key_of[4], 1), 0, SW - W - NDISP).astype(jnp.int32)
    neighbours = draw_neighbours(jax.random.fold_in(key_of[10], 71), 0)
    conv1_weight = scatter_about(key_of[6], (3, 3, 3, G, CH), (27 * G) ** -0.5, 0.4375)
    conv1_bias = scatter_about(key_of[7], (CH,), 0.5, 3.0, (), jnp.float32)
    conv2_weight = scatter_about(key_of[8], (3, 3, 3, CH, CH), (27 * CH) ** -0.5, 0.21875)
    conv2_bias = scatter_about(key_of[9], (CH,), 0.5, 3.0, (), jnp.float32)
    return {"ref_features": ref_features, "partner_lines": partner_lines, "line_owner": line_owner, "line_index": line_index, "line_offset": line_offset, "neighbours": neighbours, "conv1_weight": conv1_weight, "conv1_bias": conv1_bias, "conv2_weight": conv2_weight, "conv2_bias": conv2_bias}


def pick_rows(source, links):
    piece = source[jnp.maximum(links, 0)]
    keep = (links >= 0).reshape((-1,) + (1,) * (piece.ndim - 1))
    return jnp.where(keep, piece, jnp.zeros((), piece.dtype))


def pad_all(volume, neighbours, channels):
    tiles_count = volume.shape[0]
    deeper = jnp.pad(volume, ((0, 0), (1, 1), (0, 0), (0, 0)))
    above_row = pick_rows(deeper[:, :, H - 1, :], neighbours[:, 0])
    below_row = pick_rows(deeper[:, :, 0, :], neighbours[:, 1])
    tall_block = jnp.concatenate([above_row[:, :, None], deeper, below_row[:, :, None]], axis=2)
    grid_cells = tall_block.reshape(tiles_count, NDISP + 2, H + 2, W, channels)
    left_col = pick_rows(grid_cells[:, :, :, W - 1, :], neighbours[:, 2])
    right_col = pick_rows(grid_cells[:, :, :, 0, :], neighbours[:, 3])
    return jnp.concatenate([left_col[:, :, :, None], grid_cells, right_col[:, :, :, None]], axis=3)


def conv_all(padded, kernel):
    def single_tile(tile_block):
        output = lax.conv_general_dilated(tile_block[None], kernel, (1, 1, 1), "VALID",
                                          dimension_numbers=("NDHWC", "DHWIO", "NDHWC"),
                                          preferred_element_type=jnp.float32)
        return output[0]
    return lax.map(single_tile, padded)


def correlate(tile_features, tile_lines, tile_offsets):
    def cut_band(line_row, begin_at):
        return lax.dynamic_slice_in_dim(line_row, (begin_at * C).astype(jnp.int32), (W + NDISP) * C)
    line_bands = jax.vmap(cut_band)(tile_lines, tile_offsets).reshape(NPV, H, (W + NDISP) * C)
    features = tile_features.astype(jnp.float32)

    def one_shift(shift_step):
        window = lax.dynamic_slice_in_dim(line_bands, (shift_step * C).astype(jnp.int32), W * C, axis=2)
        product = jnp.sum(window.astype(jnp.float32) * features[None], axis=0)
        return product.reshape(H, W * G, C // G).sum(axis=2)
    return lax.map(one_shift, jnp.arange(NDISP, dtype=jnp.int32))


def reference(ref_features, partner_lines, line_owner, line_index, line_offset, neighbours,
              conv1_weight, conv1_bias, conv2_weight, conv2_bias):
    view_of = (jnp.arange(NREQ, dtype=jnp.int32) // H).astype(jnp.int32)
    lines = partner_lines[line_owner[:, :, 0], view_of[None, :], line_index]

    def tile_cost(packed):
        return correlate(packed[0], packed[1], packed[2])
    summed = lax.map(tile_cost, (ref_features, lines, line_offset))
    cost_volume = (summed * (1.0 / (NPV * (C // G)))).astype(jnp.bfloat16)
    first = conv_all(pad_all(cost_volume, neighbours, G), conv1_weight)
    hidden = jax.nn.relu(first + conv1_bias).astype(jnp.bfloat16)
    hidden = hidden.reshape(TILES, NDISP, H, W * CH)
    second = conv_all(pad_all(hidden, neighbours, CH), conv2_weight) + conv2_bias
    return second.reshape(TILES, NDISP, H, W * CH)
```

```python
from functools import partial

import jax
import jax.numpy as jnp
from jax import lax
from jax.experimental import pallas as pl
from jax.experimental.pallas import tpu as pltpu
from jax.sharding import PartitionSpec as P

C = 32
G = 8
CH = 32
NDISP = 64
W = 128
SW = 256
NPV = 4
H = 8
LANES = 128
COLS = LANES // C
LROWS = SW // COLS
WROWS = W // COLS
PITCH = WROWS + 16
HX = H + 4
FRONT = 8
LPAD = FRONT + LROWS + 8


def pack_kernel(views, lines_ref, ref_ref, req_ref, out_ref, scr):
    n_lines = lines_ref.shape[0]
    for j in range(LROWS):
        scr[pl.ds(j, n_lines, stride=LROWS), :] = lines_ref[:, j * LANES : (j + 1) * LANES].astype(jnp.float32)
    base = n_lines * LROWS
    for i in range(WROWS):
        scr[pl.ds(base + i, H, stride=WROWS), :] = ref_ref[:, i * LANES : (i + 1) * LANES].astype(jnp.float32)
    base = base + H * WROWS
    rest = scr.shape[0] - base
    scr[base:, :] = jnp.concatenate([req_ref[...], jnp.zeros((rest - req_ref.shape[0], LANES), jnp.float32)], axis=0)
    part = out_ref.shape[0]
    v = lax.axis_index("views")
    out_ref[...] = scr[pl.ds(pl.multiple_of(v * part, 16), part), :].astype(jnp.bfloat16)


def main_kernel(
    n_tiles, nd, req, nb, all_ref, w1, b1, w2, b2, gm, out_ref,
    lines, refb, linef, vt0, vte0, vt, vte, refx, x1, h2, ybuf, sem_l, sem_r,
):
    t = lax.axis_index("tiles")
    v = lax.axis_index("views")
    d0 = v * nd

    def link(x, side):
        got = nb[jnp.maximum(x, 0) * 4 + side]
        return jnp.where(x >= 0, got, -1)

    mids = [t, link(t, 2), link(t, 3)]
    tiles = [[link(m, 0), m, link(m, 1)] for m in mids]
    ref_base = NPV * H * LROWS

    spans = ((0, 2, H - 2), (2, H, 0), (H + 2, 2, 0))
    copies = []
    for s in range(3):
        for band, (at, count, row) in enumerate(spans):
            copies.append(
                pltpu.make_async_copy(
                    all_ref.at[jnp.maximum(tiles[s][band], 0), pl.ds(ref_base + row * WROWS, count * WROWS), :],
                    refb.at[s, pl.ds(at * WROWS, count * WROWS), :],
                    sem_r.at[s * 3 + band],
                )
            )
    for c in copies:
        c.start()

    def tile_of(s, hh):
        return jnp.maximum(
            jnp.where(hh < 2, tiles[s][0], jnp.where(hh < H + 2, tiles[s][1], tiles[s][2])), 0
        )

    def row_of(hh):
        return jnp.where(hh < 2, hh + H - 2, jnp.where(hh < H + 2, hh - 2, hh - H - 2))

    def fetch(hh, carry):
        row = row_of(hh)
        for s in range(3):
            tt = tile_of(s, hh)
            for u in range(NPV):
                j = tt * LANES + u * H + row
                owner = req[j]
                index = req[j + NPV * H]
                src = pl.multiple_of((u * H + index) * LROWS, LROWS)
                pltpu.make_async_copy(
                    all_ref.at[owner, pl.ds(src, LROWS), :], lines.at[s * NPV + u, hh], sem_l
                ).start()
        return carry

    lax.fori_loop(0, HX, fetch, 0)

    for c in copies:
        c.wait()
    edge = lax.broadcasted_iota(jnp.int32, (16, LANES), 0)
    for hh in range(HX):
        band = 0 if hh < 2 else (1 if hh < H + 2 else 2)
        own = refb[0, hh * WROWS : (hh + 1) * WROWS, :].astype(jnp.float32)
        refx[hh, 0:WROWS, :] = jnp.where(tiles[0][band] >= 0, own, 0.0)
        lo = refb[1, (hh + 1) * WROWS - 16 : (hh + 1) * WROWS, :].astype(jnp.float32)
        hi = refb[2, hh * WROWS : hh * WROWS + 16, :].astype(jnp.float32)
        lo = jnp.where(tiles[1][band] >= 0, lo, 0.0)
        hi = jnp.where(tiles[2][band] >= 0, hi, 0.0)
        refx[hh, WROWS:PITCH, :] = jnp.where(edge == 0, hi, jnp.where(edge == 15, lo, 0.0))

    linef[...] = jnp.zeros_like(linef)
    vt0[...] = jnp.zeros_like(vt0)
    vte0[...] = jnp.zeros_like(vte0)
    pltpu.make_async_copy(lines, lines, sem_l).wait()

    lane40 = lax.broadcasted_iota(jnp.int32, (40, LANES), 1)

    def window(buf, first, rows, r0):
        shift = lax.rem(LANES - C * r0, LANES)
        a = pltpu.roll(buf[pl.ds(first, rows), :], shift, 1)
        b = pltpu.roll(buf[pl.ds(first + 1, rows), :], shift, 1)
        return jnp.where(lane40[:rows] < LANES - C * r0, a, b)

    def assemble(hh, carry):
        row = row_of(hh)
        for s in range(3):
            tt = tile_of(s, hh)
            total = None
            for u in range(NPV):
                off = req[tt * LANES + 2 * NPV * H + u * H + row]
                col = off + d0 - 2 + FRONT * COLS
                q = lax.div(col, COLS)
                r0 = col - q * COLS
                slot = s * NPV + u
                buf = linef.at[slot]
                buf[FRONT : FRONT + LROWS, :] = lines[slot, hh].astype(jnp.float32)
                if s == 0:
                    part = window(buf, q, 40, r0)
                elif s == 1:
                    part = window(buf, q + WROWS - 1, 8, r0)
                else:
                    part = window(buf, q, 8, r0)
                total = part if total is None else total + part
            if s == 0:
                vt0[hh, 0:40, :] = total
            else:
                vte0[s - 1, hh, 0:8, :] = total
        return carry

    lax.fori_loop(0, HX, assemble, 0)

    lane1 = lax.broadcasted_iota(jnp.int32, (1, LANES), 1)

    def shift_all(hh, carry):
        for r in range(COLS):
            keep = lane1 < LANES - C * r

            def moved(x, y):
                if r == 0:
                    return x
                s = LANES - C * r
                return jnp.where(keep, pltpu.roll(x, s, 1), pltpu.roll(y, s, 1))

            vt[r, hh] = moved(vt0[hh, 0:40, :], vt0[hh, 1:41, :])
            for side in range(2):
                vte[r, side, hh] = moved(vte0[side, hh, 0:8, :], vte0[side, hh, 1:9, :])
        return carry

    lax.fori_loop(0, HX, shift_all, 0)

    lane_p = lax.broadcasted_iota(jnp.int32, (PITCH, LANES), 1)
    edge3 = lax.broadcasted_iota(jnp.int32, (16, LANES), 0) == 0
    nk = (nd + 4) // COLS
    for k in range(nk):
        def cost_row(hh, carry, k=k):
            parts = []
            ref_rows = refx[hh]
            for r in range(COLS):
                own = vt[r, hh, k : k + WROWS, :]
                side = jnp.where(edge3, vte[r, 1, hh, k : k + 1, :], vte[r, 0, hh, k : k + 1, :])
                prod = ref_rows * jnp.concatenate([own, side], axis=0)
                top = prod.astype(jnp.bfloat16)
                low = (prod - top.astype(jnp.float32)).astype(jnp.bfloat16)
                parts.append(jnp.concatenate([top, low], axis=1))
            cost = jnp.dot(jnp.concatenate(parts, axis=0), gm[...], preferred_element_type=jnp.float32)
            at = pl.multiple_of(hh * PITCH, 16)
            for r in range(COLS):
                c = cost[r * PITCH : (r + 1) * PITCH]
                x = jnp.where(
                    lane_p < COLS * G,
                    c,
                    jnp.where(lane_p < (COLS + 1) * G, pltpu.roll(c, 1, 0), pltpu.roll(c, PITCH - 1, 0)),
                )
                dd = k * COLS + r
                disp = d0 - 2 + dd
                x = jnp.where((disp >= 0) & (disp < NDISP), x, 0.0)
                x1[dd, pl.ds(at, PITCH), :] = x.astype(jnp.bfloat16)
            return carry

        lax.fori_loop(0, HX, cost_row, 0)

    rows1 = (H + 2) * PITCH
    row_id = lax.broadcasted_iota(jnp.int32, (rows1, LANES), 0)
    hrow = row_id // PITCH
    col = row_id - hrow * PITCH

    def inside(s):
        above = jnp.where(tiles[s][0] >= 0, 1, 0)
        mid = jnp.where(tiles[s][1] >= 0, 1, 0)
        below = jnp.where(tiles[s][2] >= 0, 1, 0)
        return jnp.where(hrow == 0, above, jnp.where(hrow == H + 1, below, mid))

    valid = jnp.where(col < WROWS, inside(0), jnp.where(col == WROWS, inside(2), inside(1)))
    lane_h = lax.broadcasted_iota(jnp.int32, (PITCH, LANES), 1)

    def layer1(d, carry):
        lhs = jnp.concatenate(
            [x1[d + a, b * PITCH : b * PITCH + rows1, :] for a in range(3) for b in range(3)], axis=1
        )
        y = jnp.dot(lhs, w1[...], preferred_element_type=jnp.float32)
        y = jnp.maximum(y + b1[...], 0.0)
        disp = d0 - 1 + d
        ok = jnp.where((disp >= 0) & (disp < NDISP), 1, 0)
        y = jnp.where(valid * ok > 0, y, 0.0)
        for hh in range(H + 2):
            z = y[hh * PITCH : (hh + 1) * PITCH]
            zr = pltpu.roll(z, C, 1)
            extra = jnp.where(lane_h < CH, pltpu.roll(zr, 1, 0), pltpu.roll(zr, PITCH - 1, 0))
            both = jnp.concatenate([z[:WROWS], extra[:WROWS]], axis=1)
            h2[d, hh * WROWS : (hh + 1) * WROWS, :] = both.astype(jnp.bfloat16)
        return carry

    lax.fori_loop(0, nd + 2, layer1, 0)

    rows2 = H * WROWS

    def layer2(d, carry):
        lhs = jnp.concatenate(
            [h2[d + a, b * WROWS : b * WROWS + rows2, :] for a in range(3) for b in range(3)], axis=1
        )
        ybuf[...] = jnp.dot(lhs, w2[...], preferred_element_type=jnp.float32) + b2[...]
        for i in range(WROWS):
            out_ref[d, :, i * LANES : (i + 1) * LANES] = ybuf[pl.ds(i, H, stride=WROWS), :]
        return carry

    lax.fori_loop(0, nd, layer2, 0)


def spread(kernel, depth):
    k = kernel.shape[3]
    cols = jnp.stack(
        [jnp.pad(kernel, ((0, 0), (0, 0), (j, COLS - 1 - j), (0, 0), (0, 0))) for j in range(COLS)], axis=4
    )
    cols = jnp.concatenate([cols[:, :, 1 : COLS + 1], cols[:, :, :1], cols[:, :, COLS + 1 :]], axis=2)
    mat = cols.reshape(9, (COLS + 2) * k, COLS * CH)
    mat = jnp.pad(mat, ((0, 0), (0, depth - mat.shape[1]), (0, 0)))
    return mat.reshape(9 * depth, COLS * CH)


def group_matrix():
    lane = jnp.arange(LANES)
    source = lane[:, None] // (C // G)
    target = jnp.where(
        lane < COLS * G,
        lane,
        jnp.where(
            lane < (COLS + 1) * G,
            lane - G,
            jnp.where(lane < (COLS + 2) * G, lane - (COLS + 1) * G, -1),
        ),
    )
    mat = jnp.where(source == target[None, :], 1.0 / (NPV * (C // G)), 0.0).astype(jnp.bfloat16)
    return jnp.concatenate([mat, mat], axis=0)


def on_device(
    ref_features, partner_lines, line_owner, line_index, line_offset, neighbours,
    conv1_weight, conv1_bias, conv2_weight, conv2_bias,
):
    n_tiles = lax.axis_size("tiles")
    views = lax.axis_size("views")
    nd = NDISP // views
    req = jnp.concatenate([line_owner[0, :, 0], line_index[0], line_offset[0]])
    req = jnp.pad(req, (0, LANES - req.shape[0])).astype(jnp.float32)
    req = jnp.broadcast_to(req[None], (8, LANES))
    body = NPV * H * LROWS + H * WROWS
    total = -(-(body + 16) // (16 * views)) * 16 * views
    vmem = pl.BlockSpec(memory_space=pltpu.VMEM)
    smem = pl.BlockSpec(memory_space=pltpu.SMEM)
    part = pl.pallas_call(
        partial(pack_kernel, views),
        out_shape=jax.ShapeDtypeStruct((total // views, LANES), jnp.bfloat16),
        in_specs=[vmem] * 3,
        out_specs=vmem,
        scratch_shapes=[pltpu.VMEM((total, LANES), jnp.float32)],
        compiler_params=pltpu.CompilerParams(vmem_limit_bytes=16 << 20),
        name="pack",
    )(partner_lines[0].reshape(NPV * H, SW * C), ref_features[0], req)
    gathered = lax.all_gather(part, ("tiles", "views"), axis=0, tiled=True).reshape(n_tiles, total, LANES)
    table = gathered[:, body, :].astype(jnp.int32).reshape(-1)
    nk = (nd + 4) // COLS
    f32, bf16 = jnp.float32, jnp.bfloat16
    out = pl.pallas_call(
        partial(main_kernel, n_tiles, nd),
        out_shape=jax.ShapeDtypeStruct((nd, H, W * CH), f32),
        in_specs=[smem, smem, pl.BlockSpec(memory_space=pl.ANY)] + [vmem] * 5,
        out_specs=vmem,
        scratch_shapes=[
            pltpu.VMEM((3 * NPV, HX, LROWS, LANES), bf16),
            pltpu.VMEM((3, HX * WROWS, LANES), bf16),
            pltpu.VMEM((3 * NPV, LPAD, LANES), f32),
            pltpu.VMEM((HX, 48, LANES), f32),
            pltpu.VMEM((2, HX, 16, LANES), f32),
            pltpu.VMEM((COLS, HX, 40, LANES), f32),
            pltpu.VMEM((COLS, 2, HX, 8, LANES), f32),
            pltpu.VMEM((HX, PITCH, LANES), f32),
            pltpu.VMEM((nk * COLS, HX * PITCH, LANES), bf16),
            pltpu.VMEM((nd + 2, (H + 2) * WROWS, 2 * LANES), bf16),
            pltpu.VMEM((H * WROWS, LANES), f32),
            pltpu.SemaphoreType.DMA,
            pltpu.SemaphoreType.DMA((9,)),
        ],
        compiler_params=pltpu.CompilerParams(vmem_limit_bytes=48 << 20),
        name="volume",
    )(
        table,
        neighbours.reshape(-1),
        gathered,
        spread(conv1_weight, LANES),
        jnp.tile(conv1_bias, COLS)[None],
        spread(conv2_weight, 2 * LANES),
        jnp.tile(conv2_bias, COLS)[None],
        group_matrix(),
    )
    return out[None]


def solution(mesh):
    return jax.shard_map(
        on_device,
        mesh=mesh,
        in_specs=(
            P("tiles", None, None),
            P("tiles", None, None, None),
            P("tiles", None, None),
            P("tiles", None),
            P("tiles", None),
            P(),
            P(),
            P(),
            P(),
            P(),
        ),
        out_specs=P("tiles", "views", None, None),
        check_vma=False,
    )
```

```python
from functools import partial

import jax
import jax.numpy as jnp
import numpy as np
from jax import lax
from jax.experimental import pallas as pl
from jax.experimental.pallas import tpu as pltpu
from jax.sharding import PartitionSpec as P

C = 32
G = 8
CH = 32
NDISP = 64
W = 128
SW = 256
NPV = 4
H = 8
LANES = 128
COLS = LANES // C
LROWS = SW // COLS
WROWS = W // COLS
PITCH = WROWS + 16
HX = H + 4
FRONT = 8
LPAD = FRONT + LROWS + 8
MESH = pl.DeviceIdType.MESH


def spread_taps(raw_ref, out_ref, depth):
    k = raw_ref.shape[0] // 27
    group = lax.broadcasted_iota(jnp.int32, (k, LANES), 1) // CH
    for ab in range(9):
        taps = []
        for e in range(3):
            at = (ab * 3 + e) * k
            tap = raw_ref[at : at + k, :].astype(jnp.float32)
            taps.append(jnp.concatenate([tap] * COLS, axis=1))
        rows = []
        for c in list(range(COLS)) + [-1, COLS]:
            row = jnp.zeros((k, LANES), jnp.float32)
            for e in range(3):
                row = jnp.where(group == c + 1 - e, taps[e], row)
            rows.append(row)
        rows.append(jnp.zeros((depth - len(rows) * k, LANES), jnp.float32))
        out_ref[ab * depth : (ab + 1) * depth, :] = jnp.concatenate(rows, axis=0).astype(jnp.bfloat16)


def pack_kernel(lines_ref, ref_ref, k1_ref, k2_ref, out_ref, w1_ref, w2_ref, scr):
    n_lines = lines_ref.shape[0]
    for j in range(LROWS):
        scr[pl.ds(j, n_lines, stride=LROWS), :] = lines_ref[:, j * LANES : (j + 1) * LANES].astype(jnp.float32)
    base = n_lines * LROWS
    for i in range(WROWS):
        scr[pl.ds(base + i, H, stride=WROWS), :] = ref_ref[:, i * LANES : (i + 1) * LANES].astype(jnp.float32)
    base = base + H * WROWS
    if scr.shape[0] > base:
        scr[base:, :] = jnp.zeros((scr.shape[0] - base, LANES), jnp.float32)
    part = out_ref.shape[0]
    v = lax.axis_index("views")
    out_ref[...] = scr[pl.ds(pl.multiple_of(v * part, 16), part), :].astype(jnp.bfloat16)
    spread_taps(k1_ref, w1_ref, LANES)
    spread_taps(k2_ref, w2_ref, 2 * LANES)


def gather_kernel(T, V, part_ref, req_ref, all_ref, tab_ref, own_sem, s1, r1, st, rt, s2, r2):
    t = lax.axis_index("tiles")
    v = lax.axis_index("views")
    part = part_ref.shape[0]
    hops = []
    bit = V // 2
    while bit >= 1:
        hops.append(bit)
        bit //= 2

    def flip(view, bit):
        return view + bit - 2 * bit * lax.rem(view // bit, 2)

    def partner(bit):
        return flip(v, bit)

    barrier = pltpu.get_barrier_semaphore()

    def greet(k, carry):
        peer = lax.rem(t + k, T)
        pl.semaphore_signal(barrier, inc=1, device_id=(peer, v), device_id_type=MESH)
        return carry

    lax.fori_loop(1, T, greet, 0)
    for bit in hops:
        pl.semaphore_signal(barrier, inc=1, device_id=(t, partner(bit)), device_id_type=MESH)
    pl.semaphore_wait(barrier, T - 1 + len(hops))

    def block(tile, view):
        return all_ref.at[tile, pl.ds(pl.multiple_of(view * part, 16), part), :]

    def table(peer, owner):
        return pltpu.make_async_remote_copy(
            src_ref=req_ref, dst_ref=tab_ref.at[owner], send_sem=st.at[peer], recv_sem=rt.at[owner],
            device_id=(peer, v), device_id_type=MESH,
        )

    def direct(peer, owner):
        return pltpu.make_async_remote_copy(
            src_ref=part_ref, dst_ref=block(owner, v), send_sem=s1.at[peer], recv_sem=r1.at[owner],
            device_id=(peer, v), device_id_type=MESH,
        )

    def start_direct(k, carry):
        peer = lax.rem(t + k, T)
        direct(peer, t).start()
        table(peer, t).start()
        return carry

    def forward(h, tile, view, slot):
        return pltpu.make_async_remote_copy(
            src_ref=block(tile, view), dst_ref=block(tile, view),
            send_sem=s2.at[h, slot, tile], recv_sem=r2.at[h, slot, tile],
            device_id=(t, partner(hops[h])), device_id_type=MESH,
        )

    def views_before(h):
        held = [(v, None)]
        for g in range(h):
            held = held + [(flip(view, hops[g]), (g, slot)) for slot, (view, _) in enumerate(held)]
        return held

    own_block = pltpu.make_async_copy(part_ref, block(t, v), own_sem.at[0])
    own_table = pltpu.make_async_copy(req_ref, tab_ref.at[t], own_sem.at[1])
    own_block.start()
    own_table.start()
    lax.fori_loop(1, T, start_direct, 0)
    own_block.wait()
    own_table.wait()

    n_hops = len(hops)
    final = views_before(n_hops)

    def send_on(tile, slot):
        view, came = final[slot]
        first = 0 if came is None else came[0] + 1
        for h in range(first, n_hops):
            forward(h, tile, view, slot).start()

    def land(tile, slot):
        view, came = final[slot]
        h, sent_slot = came
        forward(h, tile, view, sent_slot).wait_recv()
        send_on(tile, slot)

    def step(k, carry):
        tile = lax.rem(t - k + T, T)
        direct(tile, tile).wait_recv()
        send_on(tile, 0)
        before = lax.rem(tile + 1, T)
        for slot in range(1, len(final)):
            land(before, slot)
        return carry

    send_on(t, 0)
    lax.fori_loop(1, T, step, 0)
    last = lax.rem(t + 1, T)
    for slot in range(1, len(final)):
        land(last, slot)

    def finish(k, carry):
        tile = lax.rem(t + k, T)
        direct(tile, t).wait_send()
        table(tile, t).wait_send()
        table(tile, tile).wait_recv()
        return carry

    lax.fori_loop(1, T, finish, 0)

    def finish_forward(tile, carry):
        for slot in range(len(final)):
            view, came = final[slot]
            first = 0 if came is None else came[0] + 1
            for h in range(first, n_hops):
                forward(h, tile, view, slot).wait_send()
        return carry

    lax.fori_loop(0, T, finish_forward, 0)


def main_kernel(
    nd, nb, tab_ref, all_ref, w1, b1, w2, b2, gm, out_ref,
    tab, lines, refb, linef, vt0, vte0, vt, vte, refx, x1, h2, ybuf, sem_l, sem_r, sem_t,
):
    table_copy = pltpu.make_async_copy(tab_ref, tab, sem_t)
    table_copy.start()
    t = lax.axis_index("tiles")
    v = lax.axis_index("views")
    d0 = v * nd

    def link(x, side):
        got = nb[jnp.maximum(x, 0) * 4 + side]
        return jnp.where(x >= 0, got, -1)

    mids = [t, link(t, 2), link(t, 3)]
    tiles = [[link(m, 0), m, link(m, 1)] for m in mids]
    ref_base = NPV * H * LROWS

    spans = ((0, 2, H - 2), (2, H, 0), (H + 2, 2, 0))
    copies = []
    for s in range(3):
        for band, (at, count, row) in enumerate(spans):
            copies.append(
                pltpu.make_async_copy(
                    all_ref.at[jnp.maximum(tiles[s][band], 0), pl.ds(ref_base + row * WROWS, count * WROWS), :],
                    refb.at[s, pl.ds(at * WROWS, count * WROWS), :],
                    sem_r.at[s * 3 + band],
                )
            )
    for c in copies:
        c.start()

    def tile_of(s, hh):
        return jnp.maximum(
            jnp.where(hh < 2, tiles[s][0], jnp.where(hh < H + 2, tiles[s][1], tiles[s][2])), 0
        )

    def row_of(hh):
        return jnp.where(hh < 2, hh + H - 2, jnp.where(hh < H + 2, hh - 2, hh - H - 2))

    table_copy.wait()

    def fetch(hh, carry):
        row = row_of(hh)
        for s in range(3):
            tt = tile_of(s, hh)
            for u in range(NPV):
                owner = tab[tt, 0, u * H + row]
                index = tab[tt, 0, NPV * H + u * H + row]
                src = pl.multiple_of((u * H + index) * LROWS, LROWS)
                pltpu.make_async_copy(
                    all_ref.at[owner, pl.ds(src, LROWS), :], lines.at[s * NPV + u, hh], sem_l
                ).start()
        return carry

    lax.fori_loop(0, HX, fetch, 0)

    for c in copies:
        c.wait()
    edge = lax.broadcasted_iota(jnp.int32, (16, LANES), 0)
    for hh in range(HX):
        band = 0 if hh < 2 else (1 if hh < H + 2 else 2)
        own = refb[0, hh * WROWS : (hh + 1) * WROWS, :].astype(jnp.float32)
        refx[hh, 0:WROWS, :] = jnp.where(tiles[0][band] >= 0, own, 0.0)
        lo = refb[1, (hh + 1) * WROWS - 16 : (hh + 1) * WROWS, :].astype(jnp.float32)
        hi = refb[2, hh * WROWS : hh * WROWS + 16, :].astype(jnp.float32)
        lo = jnp.where(tiles[1][band] >= 0, lo, 0.0)
        hi = jnp.where(tiles[2][band] >= 0, hi, 0.0)
        refx[hh, WROWS:PITCH, :] = jnp.where(edge == 0, hi, jnp.where(edge == 15, lo, 0.0))

    linef[...] = jnp.zeros_like(linef)
    vt0[...] = jnp.zeros_like(vt0)
    vte0[...] = jnp.zeros_like(vte0)
    pltpu.make_async_copy(lines, lines, sem_l).wait()

    lane40 = lax.broadcasted_iota(jnp.int32, (40, LANES), 1)

    def window(buf, first, rows, r0):
        shift = lax.rem(LANES - C * r0, LANES)
        a = pltpu.roll(buf[pl.ds(first, rows), :], shift, 1)
        b = pltpu.roll(buf[pl.ds(first + 1, rows), :], shift, 1)
        return jnp.where(lane40[:rows] < LANES - C * r0, a, b)

    def assemble(hh, carry):
        row = row_of(hh)
        for s in range(3):
            tt = tile_of(s, hh)
            total = None
            for u in range(NPV):
                off = tab[tt, 0, 2 * NPV * H + u * H + row]
                col = off + d0 - 2 + FRONT * COLS
                q = lax.div(col, COLS)
                r0 = col - q * COLS
                slot = s * NPV + u
                buf = linef.at[slot]
                buf[FRONT : FRONT + LROWS, :] = lines[slot, hh].astype(jnp.float32)
                if s == 0:
                    part = window(buf, q, 40, r0)
                elif s == 1:
                    part = window(buf, q + WROWS - 1, 8, r0)
                else:
                    part = window(buf, q, 8, r0)
                total = part if total is None else total + part
            if s == 0:
                vt0[hh, 0:40, :] = total
            else:
                vte0[s - 1, hh, 0:8, :] = total
        return carry

    lax.fori_loop(0, HX, assemble, 0)

    lane1 = lax.broadcasted_iota(jnp.int32, (1, LANES), 1)

    lane_p = lax.broadcasted_iota(jnp.int32, (PITCH, LANES), 1)
    edge3 = lax.broadcasted_iota(jnp.int32, (16, LANES), 0) == 0
    nk = (nd + 4) // COLS

    def cost_row(hh, carry):
        for r in range(COLS):
            keep = lane1 < LANES - C * r

            def moved(x, y):
                if r == 0:
                    return x
                s = LANES - C * r
                return jnp.where(keep, pltpu.roll(x, s, 1), pltpu.roll(y, s, 1))

            vt[r] = moved(vt0[hh, 0:40, :], vt0[hh, 1:41, :])
            for side in range(2):
                vte[r, side] = moved(vte0[side, hh, 0:8, :], vte0[side, hh, 1:9, :])
        ref_rows = refx[hh]
        at = pl.multiple_of(hh * PITCH, 16)
        for k in range(nk):
            parts = []
            for r in range(COLS):
                own = vt[r, k : k + WROWS, :]
                side = jnp.where(edge3, vte[r, 1, k : k + 1, :], vte[r, 0, k : k + 1, :])
                prod = ref_rows * jnp.concatenate([own, side], axis=0)
                top = prod.astype(jnp.bfloat16)
                low = (prod - top.astype(jnp.float32)).astype(jnp.bfloat16)
                parts.append(jnp.concatenate([top, low], axis=1))
            cost = jnp.dot(jnp.concatenate(parts, axis=0), gm[...], preferred_element_type=jnp.float32)
            for r in range(COLS):
                c = cost[r * PITCH : (r + 1) * PITCH]
                x = jnp.where(
                    lane_p < COLS * G,
                    c,
                    jnp.where(lane_p < (COLS + 1) * G, pltpu.roll(c, 1, 0), pltpu.roll(c, PITCH - 1, 0)),
                )
                dd = k * COLS + r
                disp = d0 - 2 + dd
                x = jnp.where((disp >= 0) & (disp < NDISP), x, 0.0)
                x1[dd, pl.ds(at, PITCH), :] = x.astype(jnp.bfloat16)
        return carry

    lax.fori_loop(0, HX, cost_row, 0)

    rows1 = (H + 2) * PITCH
    row_id = lax.broadcasted_iota(jnp.int32, (rows1, LANES), 0)
    hrow = row_id // PITCH
    col = row_id - hrow * PITCH

    def inside(s):
        above = jnp.where(tiles[s][0] >= 0, 1, 0)
        mid = jnp.where(tiles[s][1] >= 0, 1, 0)
        below = jnp.where(tiles[s][2] >= 0, 1, 0)
        return jnp.where(hrow == 0, above, jnp.where(hrow == H + 1, below, mid))

    valid = jnp.where(col < WROWS, inside(0), jnp.where(col == WROWS, inside(2), inside(1)))
    lane_h = lax.broadcasted_iota(jnp.int32, (PITCH, LANES), 1)

    def layer1(d, carry):
        lhs = jnp.concatenate(
            [x1[d + a, b * PITCH : b * PITCH + rows1, :] for a in range(3) for b in range(3)], axis=1
        )
        y = jnp.dot(lhs, w1[...], preferred_element_type=jnp.float32)
        y = jnp.maximum(y + b1[...], 0.0)
        disp = d0 - 1 + d
        ok = jnp.where((disp >= 0) & (disp < NDISP), 1, 0)
        y = jnp.where(valid * ok > 0, y, 0.0)
        for hh in range(H + 2):
            z = y[hh * PITCH : (hh + 1) * PITCH]
            zr = pltpu.roll(z, C, 1)
            extra = jnp.where(lane_h < CH, pltpu.roll(zr, 1, 0), pltpu.roll(zr, PITCH - 1, 0))
            both = jnp.concatenate([z[:WROWS], extra[:WROWS]], axis=1)
            h2[d, hh * WROWS : (hh + 1) * WROWS, :] = both.astype(jnp.bfloat16)
        return carry

    def layer1_pair(i, carry):
        layer1(2 * i, carry)
        layer1(2 * i + 1, carry)
        return carry

    lax.fori_loop(0, (nd + 2) // 2, layer1_pair, 0)

    rows2 = H * WROWS

    def layer2(d, slot):
        lhs = jnp.concatenate(
            [h2[d + a, b * WROWS : b * WROWS + rows2, :] for a in range(3) for b in range(3)], axis=1
        )
        y = ybuf.at[slot]
        y[...] = jnp.dot(lhs, w2[...], preferred_element_type=jnp.float32) + b2[...]
        for i in range(WROWS):
            out_ref[d, :, i * LANES : (i + 1) * LANES] = y[pl.ds(i, H, stride=WROWS), :]

    def layer2_pair(i, carry):
        layer2(2 * i, 0)
        layer2(2 * i + 1, 1)
        return carry

    lax.fori_loop(0, nd // 2, layer2_pair, 0)


def group_matrix():
    lane = np.arange(LANES)
    source = lane[:, None] // (C // G)
    target = np.full((LANES,), -1)
    own = COLS * G
    target[:own] = lane[:own]
    target[own : own + G] = lane[own - G : own]
    target[own + G : own + 2 * G] = lane[:G]
    mat = np.where(source == target[None, :], 1.0 / (NPV * (C // G)), 0.0)
    return jnp.asarray(np.concatenate([mat, mat], axis=0), jnp.bfloat16)


def on_device(
    ref_features, partner_lines, line_owner, line_index, line_offset, neighbours,
    conv1_weight, conv1_bias, conv2_weight, conv2_bias,
):
    n_tiles = lax.axis_size("tiles")
    views = lax.axis_size("views")
    nd = NDISP // views
    req = jnp.concatenate([line_owner[0, :, 0], line_index[0], line_offset[0]])
    req = jnp.broadcast_to(jnp.pad(req, (0, LANES - req.shape[0]))[None], (8, LANES))
    body = NPV * H * LROWS + H * WROWS
    total = -(-body // (16 * views)) * 16 * views
    vmem = pl.BlockSpec(memory_space=pltpu.VMEM)
    smem = pl.BlockSpec(memory_space=pltpu.SMEM)
    hbm = pl.BlockSpec(memory_space=pl.ANY)
    part, w1, w2 = pl.pallas_call(
        pack_kernel,
        out_shape=[
            jax.ShapeDtypeStruct((total // views, LANES), jnp.bfloat16),
            jax.ShapeDtypeStruct((9 * LANES, LANES), jnp.bfloat16),
            jax.ShapeDtypeStruct((18 * LANES, LANES), jnp.bfloat16),
        ],
        in_specs=[vmem] * 4,
        out_specs=[vmem] * 3,
        scratch_shapes=[pltpu.VMEM((total, LANES), jnp.float32)],
        compiler_params=pltpu.CompilerParams(vmem_limit_bytes=16 << 20),
        name="pack",
    )(
        partner_lines[0].reshape(NPV * H, SW * C),
        ref_features[0],
        conv1_weight.reshape(27 * G, CH),
        conv2_weight.reshape(27 * CH, CH),
    )
    hops = max(1, views.bit_length() - 1)
    dma = pltpu.SemaphoreType.DMA
    gathered, table = pl.pallas_call(
        partial(gather_kernel, n_tiles, views),
        out_shape=[
            jax.ShapeDtypeStruct((n_tiles, total, LANES), jnp.bfloat16),
            jax.ShapeDtypeStruct((n_tiles, 8, LANES), jnp.int32),
        ],
        in_specs=[hbm, hbm],
        out_specs=[hbm, hbm],
        scratch_shapes=[
            dma((2,)), dma((n_tiles,)), dma((n_tiles,)), dma((n_tiles,)), dma((n_tiles,)),
            dma((hops, views, n_tiles)), dma((hops, views, n_tiles)),
        ],
        compiler_params=pltpu.CompilerParams(collective_id=0, has_side_effects=True),
        name="gather",
    )(part, req)
    nk = (nd + 4) // COLS
    f32, bf16 = jnp.float32, jnp.bfloat16
    out = pl.pallas_call(
        partial(main_kernel, nd),
        out_shape=jax.ShapeDtypeStruct((nd, H, W * CH), f32),
        in_specs=[smem, hbm, hbm] + [vmem] * 5,
        out_specs=vmem,
        scratch_shapes=[
            pltpu.SMEM((n_tiles, 8, LANES), jnp.int32),
            pltpu.VMEM((3 * NPV, HX, LROWS, LANES), bf16),
            pltpu.VMEM((3, HX * WROWS, LANES), bf16),
            pltpu.VMEM((3 * NPV, LPAD, LANES), f32),
            pltpu.VMEM((HX, 48, LANES), f32),
            pltpu.VMEM((2, HX, 16, LANES), f32),
            pltpu.VMEM((COLS, 40, LANES), f32),
            pltpu.VMEM((COLS, 2, 8, LANES), f32),
            pltpu.VMEM((HX, PITCH, LANES), f32),
            pltpu.VMEM((nk * COLS, HX * PITCH, LANES), bf16),
            pltpu.VMEM((nd + 2, (H + 2) * WROWS, 2 * LANES), bf16),
            pltpu.VMEM((2, H * WROWS, LANES), f32),
            dma,
            dma((9,)),
            dma,
        ],
        compiler_params=pltpu.CompilerParams(vmem_limit_bytes=48 << 20),
        name="volume",
    )(
        neighbours.reshape(-1),
        table,
        gathered,
        w1,
        jnp.tile(conv1_bias, COLS)[None],
        w2,
        jnp.tile(conv2_bias, COLS)[None],
        group_matrix(),
    )
    return out[None]


def solution(mesh):
    return jax.shard_map(
        on_device,
        mesh=mesh,
        in_specs=(
            P("tiles", None, None),
            P("tiles", None, None, None),
            P("tiles", None, None),
            P("tiles", None),
            P("tiles", None),
            P(),
            P(),
            P(),
            P(),
            P(),
        ),
        out_specs=P("tiles", "views", None, None),
        check_vma=False,
    )
```

```python
import heapq
from functools import partial

import jax
import jax.numpy as jnp
from jax import lax
from jax.experimental import pallas as pl
from jax.experimental.pallas import tpu as pltpu
from jax.sharding import PartitionSpec as P

C = 32
G = 8
CH = 32
NDISP = 64
W = 128
SW = 256
NPV = 4
H = 8
LANES = 128
COLS = LANES // C
LROWS = SW // COLS
WROWS = W // COLS
PITCH = WROWS + 16
HX = H + 4
FRONT = 8
LPAD = FRONT + LROWS + 8
MESH = pl.DeviceIdType.MESH


def spread_taps(raw_ref, out_ref, depth, pitch):
    k = raw_ref.shape[0] // 27
    group = lax.broadcasted_iota(jnp.int32, (k, LANES), 1) // CH
    for ab in range(9):
        taps = []
        for e in range(3):
            at = (ab * 3 + e) * k
            tap = raw_ref[at : at + k, :].astype(jnp.float32)
            taps.append(jnp.concatenate([tap] * COLS, axis=1))
        rows = []
        for c in list(range(COLS)) + [-1, COLS]:
            row = jnp.zeros((k, LANES), jnp.float32)
            for e in range(3):
                row = jnp.where(group == c + 1 - e, taps[e], row)
            rows.append(row)
        rows.append(jnp.zeros((depth - len(rows) * k, LANES), jnp.float32))
        at = ab // 3 * pitch + ab % 3 * depth
        out_ref[at : at + depth, :] = jnp.concatenate(rows, axis=0).astype(jnp.bfloat16)
    if pitch > 3 * depth:
        for a in range(3):
            out_ref[a * pitch + 3 * depth : (a + 1) * pitch, :] = jnp.zeros((pitch - 3 * depth, LANES), jnp.bfloat16)


def pack_kernel(lines_ref, ref_ref, k1_ref, k2_ref, req_ref, out_ref, w1_ref, w2_ref, req8_ref, scr):
    req8_ref[...] = jnp.broadcast_to(req_ref[...], req8_ref.shape)
    n_lines = lines_ref.shape[0]
    for j in range(LROWS):
        scr[pl.ds(j, n_lines, stride=LROWS), :] = lines_ref[:, j * LANES : (j + 1) * LANES].astype(jnp.float32)
    base = n_lines * LROWS
    for i in range(WROWS):
        scr[pl.ds(base + i, H, stride=WROWS), :] = ref_ref[:, i * LANES : (i + 1) * LANES].astype(jnp.float32)
    base = base + H * WROWS
    if scr.shape[0] > base:
        scr[base:, :] = jnp.zeros((scr.shape[0] - base, LANES), jnp.float32)
    part = out_ref.shape[0]
    v = lax.axis_index("views")
    out_ref[...] = scr[pl.ds(pl.multiple_of(v * part, 16), part), :].astype(jnp.bfloat16)
    spread_taps(k1_ref, w1_ref, LANES // 2, 2 * LANES)
    spread_taps(k2_ref, w2_ref, 2 * LANES, 6 * LANES)


def hop_orders(T, V):
    def bits(axis, size):
        out = []
        while size > 1:
            size //= 2
            out.append((axis, size))
        return out

    tb, vb = bits(0, T), bits(1, V)
    first = tb + vb
    second = tb[:-1] + vb[:1] + tb[-1:] + vb[1:]
    return first, second, tb


def arrivals(orders, costs):
    free = {}
    heap = [(0.0, o, 0) for o in range(len(orders))]
    seen = []
    while heap:
        now, o, mask = heapq.heappop(heap)
        seen.append((o, mask))
        for h in range(mask.bit_length(), len(orders[o])):
            hop = orders[o][h]
            free[hop] = max(free.get(hop, 0.0), now) + costs[o] * (0.2 if hop == (1, 1) else 1.0)
            heapq.heappush(heap, (free[hop], o, mask | (1 << h)))
    return seen


def gather_kernel(T, V, part_ref, req_ref, all_ref, tab_ref, own_sem, *sems):
    t = lax.axis_index("tiles")
    v = lax.axis_index("views")
    part = part_ref.shape[0]
    half = part // 2
    orders = hop_orders(T, V)

    def flip(x, bit):
        return x + bit - 2 * bit * lax.rem(lax.div(x, bit), 2)

    def across(mask, order):
        at = [t, v]
        for h, (axis, bit) in enumerate(order):
            if mask >> h & 1:
                at[axis] = flip(at[axis], bit)
        return tuple(at)

    barrier = pltpu.get_barrier_semaphore()
    hops = orders[0]
    for hop in hops:
        pl.semaphore_signal(barrier, inc=1, device_id=across(1, [hop]), device_id_type=MESH)
    pl.semaphore_wait(barrier, len(hops))

    def place(o, mask):
        tile, view = across(mask, orders[o])
        if o == 2:
            return tab_ref.at[tile]
        return all_ref.at[tile, pl.ds(pl.multiple_of(view * part + o * half, 16), half), :]

    def source(o):
        return req_ref if o == 2 else part_ref.at[pl.ds(o * half, half), :]

    def send(o, mask, h):
        return pltpu.make_async_remote_copy(
            src_ref=source(o) if mask == 0 else place(o, mask),
            dst_ref=place(o, mask),
            send_sem=sems[2 * o].at[mask | (1 << h)],
            recv_sem=sems[2 * o + 1].at[mask | (1 << h)],
            device_id=across(1 << h, orders[o]),
            device_id_type=MESH,
        )

    def landed(o, mask):
        return pltpu.make_async_remote_copy(
            src_ref=place(o, mask),
            dst_ref=place(o, mask),
            send_sem=sems[2 * o].at[mask],
            recv_sem=sems[2 * o + 1].at[mask],
            device_id=across(1, orders[o]),
            device_id_type=MESH,
        )

    sent = []
    own = []
    for o, mask in arrivals(orders, (1.0, 1.0, 0.02)):
        if mask:
            landed(o, mask).wait_recv()
        for h in range(mask.bit_length(), len(orders[o])):
            copy = send(o, mask, h)
            copy.start()
            sent.append(copy)
        if mask == 0:
            mine = pltpu.make_async_copy(source(o), place(o, 0), own_sem.at[o])
            mine.start()
            own.append(mine)
    for copy in own:
        copy.wait()
    for copy in sent:
        copy.wait_send()


def main_kernel(
    nd, nb, tab_ref, all_ref, w1, b1, w2, b2, out_ref,
    tab, lines, refb, linef, vt0, vte0, vt, vte, refx, xprev, x1, h2, ybuf, sem_l, sem_r, sem_t,
):
    table_copy = pltpu.make_async_copy(tab_ref, tab, sem_t)
    table_copy.start()
    t = lax.axis_index("tiles")
    v = lax.axis_index("views")
    d0 = v * nd

    def link(x, side):
        got = nb[jnp.maximum(x, 0), side]
        return jnp.where(x >= 0, got, -1)

    mids = [t, link(t, 2), link(t, 3)]
    tiles = [[link(m, 0), m, link(m, 1)] for m in mids]
    ref_base = NPV * H * LROWS

    spans = ((0, 2, H - 2), (2, H, 0), (H + 2, 2, 0))
    copies = []
    for s in range(3):
        for band, (at, count, row) in enumerate(spans):
            copies.append(
                pltpu.make_async_copy(
                    all_ref.at[jnp.maximum(tiles[s][band], 0), pl.ds(ref_base + row * WROWS, count * WROWS), :],
                    refb.at[s, pl.ds(at * WROWS, count * WROWS), :],
                    sem_r.at[s * 3 + band],
                )
            )
    for c in copies:
        c.start()

    def tile_of(s, hh):
        return jnp.maximum(
            jnp.where(hh < 2, tiles[s][0], jnp.where(hh < H + 2, tiles[s][1], tiles[s][2])), 0
        )

    def row_of(hh):
        return jnp.where(hh < 2, hh + H - 2, jnp.where(hh < H + 2, hh - 2, hh - H - 2))

    table_copy.wait()

    def fetch(hh, carry):
        row = row_of(hh)
        for s in range(3):
            tt = tile_of(s, hh)
            for u in range(NPV):
                owner = tab[tt, 0, u * H + row]
                index = tab[tt, 0, NPV * H + u * H + row]
                src = pl.multiple_of((u * H + index) * LROWS, LROWS)
                pltpu.make_async_copy(
                    all_ref.at[owner, pl.ds(src, LROWS), :], lines.at[s * NPV + u, hh], sem_l
                ).start()
        return carry

    lax.fori_loop(0, HX, fetch, 0)

    for c in copies:
        c.wait()
    edge = lax.broadcasted_iota(jnp.int32, (16, LANES), 0)
    for hh in range(HX):
        band = 0 if hh < 2 else (1 if hh < H + 2 else 2)
        own = refb[0, hh * WROWS : (hh + 1) * WROWS, :].astype(jnp.float32)
        refx[hh, 0:WROWS, :] = jnp.where(tiles[0][band] >= 0, own, 0.0)
        lo = refb[1, (hh + 1) * WROWS - 16 : (hh + 1) * WROWS, :].astype(jnp.float32)
        hi = refb[2, hh * WROWS : hh * WROWS + 16, :].astype(jnp.float32)
        lo = jnp.where(tiles[1][band] >= 0, lo, 0.0)
        hi = jnp.where(tiles[2][band] >= 0, hi, 0.0)
        refx[hh, WROWS:PITCH, :] = jnp.where(edge == 0, hi, jnp.where(edge == 15, lo, 0.0))

    linef[...] = jnp.zeros_like(linef)
    vt0[...] = jnp.zeros_like(vt0)
    vte0[...] = jnp.zeros_like(vte0)
    pltpu.make_async_copy(lines, lines, sem_l).wait()

    lane40 = lax.broadcasted_iota(jnp.int32, (40, LANES), 1)

    def window(buf, first, rows, r0):
        shift = lax.rem(LANES - C * r0, LANES)
        a = pltpu.roll(buf[pl.ds(first, rows), :], shift, 1)
        b = pltpu.roll(buf[pl.ds(first + 1, rows), :], shift, 1)
        return jnp.where(lane40[:rows] < LANES - C * r0, a, b)

    def assemble(hh, carry):
        row = row_of(hh)
        for s in range(3):
            tt = tile_of(s, hh)
            total = None
            for u in range(NPV):
                off = tab[tt, 0, 2 * NPV * H + u * H + row]
                col = off + d0 - 2 + FRONT * COLS
                q = lax.div(col, COLS)
                r0 = col - q * COLS
                slot = s * NPV + u
                buf = linef.at[slot]
                buf[FRONT : FRONT + LROWS, :] = lines[slot, hh].astype(jnp.float32)
                if s == 0:
                    part = window(buf, q, 40, r0)
                elif s == 1:
                    part = window(buf, q + WROWS - 1, 8, r0)
                else:
                    part = window(buf, q, 8, r0)
                total = part if total is None else total + part
            if s == 0:
                vt0[hh, 0:40, :] = total
            else:
                vte0[s - 1, hh, 0:8, :] = total
        return carry

    lax.fori_loop(0, HX, assemble, 0)

    lane1 = lax.broadcasted_iota(jnp.int32, (1, LANES), 1)

    lane_p = lax.broadcasted_iota(jnp.int32, (PITCH, LANES), 1)
    edge3 = lax.broadcasted_iota(jnp.int32, (16, LANES), 0) == 0
    lane_half = lax.rem(lane_p, LANES // 2)
    nk = (nd + 4) // COLS
    gm = group_matrix()

    def cost_row(hh, carry):
        for r in range(COLS):
            keep = lane1 < LANES - C * r

            def moved(x, y):
                if r == 0:
                    return x
                s = LANES - C * r
                return jnp.where(keep, pltpu.roll(x, s, 1), pltpu.roll(y, s, 1))

            vt[r] = moved(vt0[hh, 0:40, :], vt0[hh, 1:41, :])
            for side in range(2):
                vte[r, side] = moved(vte0[side, hh, 0:8, :], vte0[side, hh, 1:9, :])
        ref_rows = refx[hh]
        at = pl.multiple_of(hh * PITCH, 16)
        for k in range(nk):
            parts = []
            for r in range(COLS):
                own = vt[r, k : k + WROWS, :]
                side = jnp.where(edge3, vte[r, 1, k : k + 1, :], vte[r, 0, k : k + 1, :])
                prod = ref_rows * jnp.concatenate([own, side], axis=0)
                top = prod.astype(jnp.bfloat16)
                low = (prod - top.astype(jnp.float32)).astype(jnp.bfloat16)
                parts.append(jnp.concatenate([top, low], axis=1))
            cost = jnp.dot(jnp.concatenate(parts, axis=0), gm, preferred_element_type=jnp.float32)
            for r in range(COLS):
                c = cost[r * PITCH : (r + 1) * PITCH]
                x = jnp.where(
                    lane_half < COLS * G,
                    c,
                    jnp.where(lane_half < (COLS + 1) * G, pltpu.roll(c, 1, 0), pltpu.roll(c, PITCH - 1, 0)),
                )
                dd = k * COLS + r
                if dd < 2 or dd >= nd + 2:
                    disp = d0 - 2 + dd
                    x = jnp.where((disp >= 0) & (disp < NDISP), x, 0.0)
                both = jnp.where(lane_p < LANES // 2, xprev[dd], x)
                x1[dd, pl.ds(at, PITCH), :] = both.astype(jnp.bfloat16)
                xprev[dd] = x
        return carry

    lax.fori_loop(0, HX, cost_row, 0)
    for dd in range(nk * COLS):
        x1[dd, HX * PITCH : (HX + 1) * PITCH, :] = xprev[dd].astype(jnp.bfloat16)

    rows1 = (H + 2) * PITCH
    row_id = lax.broadcasted_iota(jnp.int32, (rows1, LANES), 0)
    hrow = row_id // PITCH
    col = row_id - hrow * PITCH

    def inside(s):
        above = jnp.where(tiles[s][0] >= 0, 1, 0)
        mid = jnp.where(tiles[s][1] >= 0, 1, 0)
        below = jnp.where(tiles[s][2] >= 0, 1, 0)
        return jnp.where(hrow == 0, above, jnp.where(hrow == H + 1, below, mid))

    valid = jnp.where(col < WROWS, inside(0), jnp.where(col == WROWS, inside(2), inside(1)))
    bias1 = jnp.concatenate([b1[...]] * COLS, axis=1)
    bias2 = jnp.concatenate([b2[...]] * COLS, axis=1)
    lane_h = lax.broadcasted_iota(jnp.int32, (PITCH, LANES), 1)

    def layer1(d, carry):
        lhs = jnp.concatenate(
            [x1[d + a, b * PITCH : b * PITCH + rows1, :] for a in range(3) for b in (1, 3)], axis=1
        )
        y = jnp.dot(lhs, w1[...], preferred_element_type=jnp.float32)
        y = jnp.maximum(y + bias1, 0.0)
        disp = d0 - 1 + d
        least = jnp.where((disp >= 0) & (disp < NDISP), 0, 1)
        y = jnp.where(valid > least, y, 0.0)
        for hh in range(H + 2):
            z = y[hh * PITCH : (hh + 1) * PITCH]
            zr = pltpu.roll(z, C, 1)
            extra = jnp.where(lane_h < CH, pltpu.roll(zr, 1, 0), pltpu.roll(zr, PITCH - 1, 0))
            both = jnp.concatenate([z[:WROWS], extra[:WROWS]], axis=1)
            h2[d, hh * WROWS : (hh + 1) * WROWS, :] = both.astype(jnp.bfloat16)
        return carry

    def layer1_pair(i, carry):
        layer1(2 * i, carry)
        layer1(2 * i + 1, carry)
        return carry

    lax.fori_loop(0, (nd + 2) // 2, layer1_pair, 0)

    rows2 = H * WROWS

    def layer2(d, slot):
        lhs = jnp.concatenate(
            [h2[d + a, b * WROWS : b * WROWS + rows2, :] for a in range(3) for b in range(3)], axis=1
        )
        y = ybuf.at[slot]
        y[...] = jnp.dot(lhs, w2[...], preferred_element_type=jnp.float32) + bias2
        for i in range(WROWS):
            out_ref[d, :, i * LANES : (i + 1) * LANES] = y[pl.ds(i, H, stride=WROWS), :]

    def layer2_pair(i, carry):
        layer2(2 * i, 0)
        layer2(2 * i + 1, 1)
        return carry

    lax.fori_loop(0, nd // 2, layer2_pair, 0)


def group_matrix():
    row = lax.broadcasted_iota(jnp.int32, (2 * LANES, LANES), 0)
    lane = lax.broadcasted_iota(jnp.int32, (2 * LANES, LANES), 1)
    source = lax.rem(row, LANES) // (C // G)
    lane = lax.rem(lane, LANES // 2)
    own = COLS * G
    target = jnp.where(
        lane < own, lane, jnp.where(lane < own + G, lane - G, jnp.where(lane < own + 2 * G, lane - own - G, -1))
    )
    return jnp.where(source == target, 1.0 / (NPV * (C // G)), 0.0).astype(jnp.bfloat16)


def on_device(
    ref_features, partner_lines, line_owner, line_index, line_offset, neighbours,
    conv1_weight, conv1_bias, conv2_weight, conv2_bias,
):
    n_tiles = lax.axis_size("tiles")
    views = lax.axis_size("views")
    nd = NDISP // views
    req = jnp.concatenate([line_owner[0, :, 0], line_index[0], line_offset[0]])
    req = jnp.pad(req, (0, LANES - req.shape[0]))[None]
    body = NPV * H * LROWS + H * WROWS
    total = -(-body // (32 * views)) * 32 * views
    vmem = pl.BlockSpec(memory_space=pltpu.VMEM)
    smem = pl.BlockSpec(memory_space=pltpu.SMEM)
    hbm = pl.BlockSpec(memory_space=pl.ANY)
    part, w1, w2, req8 = pl.pallas_call(
        pack_kernel,
        out_shape=[
            jax.ShapeDtypeStruct((total // views, LANES), jnp.bfloat16),
            jax.ShapeDtypeStruct((6 * LANES, LANES), jnp.bfloat16),
            jax.ShapeDtypeStruct((18 * LANES, LANES), jnp.bfloat16),
            jax.ShapeDtypeStruct((8, LANES), jnp.int32),
        ],
        in_specs=[vmem] * 5,
        out_specs=[vmem] * 4,
        scratch_shapes=[pltpu.VMEM((total, LANES), jnp.float32)],
        compiler_params=pltpu.CompilerParams(vmem_limit_bytes=60 << 20),
        name="pack",
    )(
        partner_lines[0].reshape(NPV * H, SW * C),
        ref_features[0],
        conv1_weight.reshape(27 * G, CH),
        conv2_weight.reshape(27 * CH, CH),
        req,
    )
    orders = hop_orders(n_tiles, views)
    dma = pltpu.SemaphoreType.DMA
    gathered, table = pl.pallas_call(
        partial(gather_kernel, n_tiles, views),
        out_shape=[
            jax.ShapeDtypeStruct((n_tiles, total, LANES), jnp.bfloat16),
            jax.ShapeDtypeStruct((n_tiles, 8, LANES), jnp.int32),
        ],
        in_specs=[hbm, hbm],
        out_specs=[hbm, hbm],
        scratch_shapes=[
            dma((len(orders),)),
            *[dma((1 << len(order),)) for order in orders for _ in range(2)],
        ],
        compiler_params=pltpu.CompilerParams(
            collective_id=0, has_side_effects=True, vmem_limit_bytes=60 << 20
        ),
        name="gather",
    )(part, req8)
    nk = (nd + 4) // COLS
    f32, bf16 = jnp.float32, jnp.bfloat16
    out = pl.pallas_call(
        partial(main_kernel, nd),
        out_shape=jax.ShapeDtypeStruct((nd, H, W * CH), f32),
        in_specs=[smem, hbm, hbm] + [vmem] * 4,
        out_specs=vmem,
        scratch_shapes=[
            pltpu.SMEM((n_tiles, 8, LANES), jnp.int32),
            pltpu.VMEM((3 * NPV, HX, LROWS, LANES), bf16),
            pltpu.VMEM((3, HX * WROWS, LANES), bf16),
            pltpu.VMEM((3 * NPV, LPAD, LANES), f32),
            pltpu.VMEM((HX, 48, LANES), f32),
            pltpu.VMEM((2, HX, 16, LANES), f32),
            pltpu.VMEM((COLS, 40, LANES), f32),
            pltpu.VMEM((COLS, 2, 8, LANES), f32),
            pltpu.VMEM((HX, PITCH, LANES), f32),
            pltpu.VMEM((nk * COLS, PITCH, LANES), f32),
            pltpu.VMEM((nk * COLS, (HX + 1) * PITCH, LANES), bf16),
            pltpu.VMEM((nd + 2, (H + 2) * WROWS, 2 * LANES), bf16),
            pltpu.VMEM((2, H * WROWS, LANES), f32),
            dma,
            dma((9,)),
            dma,
        ],
        compiler_params=pltpu.CompilerParams(vmem_limit_bytes=60 << 20),
        name="volume",
    )(
        neighbours,
        table,
        gathered,
        w1,
        conv1_bias[None],
        w2,
        conv2_bias[None],
    )
    return out[None]


def solution(mesh):
    return jax.shard_map(
        on_device,
        mesh=mesh,
        in_specs=(
            P("tiles", None, None),
            P("tiles", None, None, None),
            P("tiles", None, None),
            P("tiles", None),
            P("tiles", None),
            P(),
            P(),
            P(),
            P(),
            P(),
        ),
        out_specs=P("tiles", "views", None, None),
        check_vma=False,
    )
```

```python
import heapq
from functools import partial

import jax
import jax.numpy as jnp
from jax import lax
from jax.experimental import pallas as pl
from jax.experimental.pallas import tpu as pltpu
from jax.sharding import PartitionSpec as P

C = 32
G = 8
CH = 32
NDISP = 64
W = 128
SW = 256
NPV = 4
H = 8
LANES = 128
COLS = LANES // C
LROWS = SW // COLS
WROWS = W // COLS
PITCH = WROWS + 16
HX = H + 4
FRONT = 8
LPAD = FRONT + LROWS + 8
MESH = pl.DeviceIdType.MESH


def spread_taps(raw_ref, out_ref, depth, pitch):
    k = raw_ref.shape[0] // 27
    group = lax.broadcasted_iota(jnp.int32, (k, LANES), 1) // CH
    for ab in range(9):
        taps = []
        for e in range(3):
            at = (ab * 3 + e) * k
            tap = raw_ref[at : at + k, :].astype(jnp.float32)
            taps.append(jnp.concatenate([tap] * COLS, axis=1))
        rows = []
        for c in list(range(COLS)) + [-1, COLS]:
            row = jnp.zeros((k, LANES), jnp.float32)
            for e in range(3):
                row = jnp.where(group == c + 1 - e, taps[e], row)
            rows.append(row)
        rows.append(jnp.zeros((depth - len(rows) * k, LANES), jnp.float32))
        at = ab // 3 * pitch + ab % 3 * depth
        out_ref[at : at + depth, :] = jnp.concatenate(rows, axis=0).astype(jnp.bfloat16)
    if pitch > 3 * depth:
        for a in range(3):
            out_ref[a * pitch + 3 * depth : (a + 1) * pitch, :] = jnp.zeros((pitch - 3 * depth, LANES), jnp.bfloat16)


def pack_own(lines_ref, ref_ref, scr, part_ref):
    n_lines = lines_ref.shape[0]
    for j in range(LROWS):
        scr[pl.ds(j, n_lines, stride=LROWS), :] = lines_ref[:, j * LANES : (j + 1) * LANES].astype(jnp.float32)
    base = n_lines * LROWS
    for i in range(WROWS):
        scr[pl.ds(base + i, H, stride=WROWS), :] = ref_ref[:, i * LANES : (i + 1) * LANES].astype(jnp.float32)
    base = base + H * WROWS
    if scr.shape[0] > base:
        scr[base:, :] = jnp.zeros((scr.shape[0] - base, LANES), jnp.float32)
    part = part_ref.shape[0]
    v = lax.axis_index("views")
    part_ref[...] = scr[pl.ds(pl.multiple_of(v * part, 16), part), :].astype(jnp.bfloat16)


def hop_orders(T, V):
    def bits(axis, size):
        out = []
        while size > 1:
            size //= 2
            out.append((axis, size))
        return out

    tb, vb = bits(0, T), bits(1, V)
    first = tb + vb
    second = tb[:-1] + vb[:1] + tb[-1:] + vb[1:]
    return first, second, tb


def arrivals(orders, costs):
    free = {}
    heap = [(0.0, o, 0) for o in range(len(orders))]
    seen = []
    while heap:
        now, o, mask = heapq.heappop(heap)
        seen.append((o, mask))
        for h in range(mask.bit_length(), len(orders[o])):
            hop = orders[o][h]
            free[hop] = max(free.get(hop, 0.0), now) + costs[o] * (0.2 if hop == (1, 1) else 1.0)
            heapq.heappush(heap, (free[hop], o, mask | (1 << h)))
    return seen


def gather_kernel(
    T, V, lines_ref, ref_ref, owner_ref, index_ref, offset_ref, k1_ref, k2_ref,
    all_ref, tab_ref, w1_ref, w2_ref, scr, part_ref, req_ref, own_sem, *sems
):
    t = lax.axis_index("tiles")
    v = lax.axis_index("views")
    part = part_ref.shape[0]
    half = part // 2
    orders = hop_orders(T, V)

    def flip(x, bit):
        return x + bit - 2 * bit * lax.rem(lax.div(x, bit), 2)

    def across(mask, order):
        at = [t, v]
        for h, (axis, bit) in enumerate(order):
            if mask >> h & 1:
                at[axis] = flip(at[axis], bit)
        return tuple(at)

    barrier = pltpu.get_barrier_semaphore()
    hops = orders[0]
    for hop in hops:
        pl.semaphore_signal(barrier, inc=1, device_id=across(1, [hop]), device_id_type=MESH)
    pack_own(lines_ref, ref_ref, scr, part_ref)
    asked = [owner_ref[...], index_ref[...], offset_ref[...]]
    asked.append(jnp.zeros((1, LANES - 3 * asked[0].shape[1]), jnp.int32))
    req_ref[...] = jnp.broadcast_to(jnp.concatenate(asked, axis=1), req_ref.shape)
    pl.semaphore_wait(barrier, len(hops))

    def place(o, mask):
        tile, view = across(mask, orders[o])
        if o == 2:
            return tab_ref.at[tile]
        return all_ref.at[tile, pl.ds(pl.multiple_of(view * part + o * half, 16), half), :]

    def source(o):
        return req_ref if o == 2 else part_ref.at[pl.ds(o * half, half), :]

    def send(o, mask, h):
        return pltpu.make_async_remote_copy(
            src_ref=source(o) if mask == 0 else place(o, mask),
            dst_ref=place(o, mask),
            send_sem=sems[2 * o].at[mask | (1 << h)],
            recv_sem=sems[2 * o + 1].at[mask | (1 << h)],
            device_id=across(1 << h, orders[o]),
            device_id_type=MESH,
        )

    def landed(o, mask):
        return pltpu.make_async_remote_copy(
            src_ref=place(o, mask),
            dst_ref=place(o, mask),
            send_sem=sems[2 * o].at[mask],
            recv_sem=sems[2 * o + 1].at[mask],
            device_id=across(1, orders[o]),
            device_id_type=MESH,
        )

    sent = []
    own = []
    spread = False
    for o, mask in arrivals(orders, (1.0, 1.0, 0.02)):
        if mask and not spread:
            spread_taps(k1_ref, w1_ref, LANES // 2, 2 * LANES)
            spread_taps(k2_ref, w2_ref, 2 * LANES, 6 * LANES)
            spread = True
        if mask:
            landed(o, mask).wait_recv()
        for h in range(mask.bit_length(), len(orders[o])):
            copy = send(o, mask, h)
            copy.start()
            sent.append(copy)
        if mask == 0:
            mine = pltpu.make_async_copy(source(o), place(o, 0), own_sem.at[o])
            mine.start()
            own.append(mine)
    for copy in own:
        copy.wait()
    for copy in sent:
        copy.wait_send()


def main_kernel(
    nd, nb, tab_ref, all_ref, w1, b1, w2, b2, out_ref,
    tab, lines, refb, linef, vt0, vte0, vt, vte, refx, xprev, x1, h2, ybuf, sem_l, sem_r, sem_t,
):
    table_copy = pltpu.make_async_copy(tab_ref, tab, sem_t)
    table_copy.start()
    t = lax.axis_index("tiles")
    v = lax.axis_index("views")
    d0 = v * nd

    def link(x, side):
        got = nb[side, jnp.maximum(x, 0)]
        return jnp.where(x >= 0, got, -1)

    mids = [t, link(t, 2), link(t, 3)]
    tiles = [[link(m, 0), m, link(m, 1)] for m in mids]
    ref_base = NPV * H * LROWS

    spans = ((0, 2, H - 2), (2, H, 0), (H + 2, 2, 0))
    copies = []
    for s in range(3):
        for band, (at, count, row) in enumerate(spans):
            copies.append(
                pltpu.make_async_copy(
                    all_ref.at[jnp.maximum(tiles[s][band], 0), pl.ds(ref_base + row * WROWS, count * WROWS), :],
                    refb.at[s, pl.ds(at * WROWS, count * WROWS), :],
                    sem_r.at[s * 3 + band],
                )
            )
    for c in copies:
        c.start()

    def tile_of(s, hh):
        return jnp.maximum(
            jnp.where(hh < 2, tiles[s][0], jnp.where(hh < H + 2, tiles[s][1], tiles[s][2])), 0
        )

    def row_of(hh):
        return jnp.where(hh < 2, hh + H - 2, jnp.where(hh < H + 2, hh - 2, hh - H - 2))

    table_copy.wait()

    def fetch(hh, carry):
        row = row_of(hh)
        for s in range(3):
            tt = tile_of(s, hh)
            for u in range(NPV):
                owner = tab[tt, 0, u * H + row]
                index = tab[tt, 0, NPV * H + u * H + row]
                src = pl.multiple_of((u * H + index) * LROWS, LROWS)
                pltpu.make_async_copy(
                    all_ref.at[owner, pl.ds(src, LROWS), :], lines.at[hh, s * NPV + u], sem_l.at[hh]
                ).start()
        return carry

    ahead = 4
    lax.fori_loop(0, ahead, fetch, 0)

    for c in copies:
        c.wait()
    edge = lax.broadcasted_iota(jnp.int32, (16, LANES), 0)
    for hh in range(HX):
        band = 0 if hh < 2 else (1 if hh < H + 2 else 2)
        own = refb[0, hh * WROWS : (hh + 1) * WROWS, :].astype(jnp.float32)
        refx[hh, 0:WROWS, :] = jnp.where(tiles[0][band] >= 0, own, 0.0)
        lo = refb[1, (hh + 1) * WROWS - 16 : (hh + 1) * WROWS, :].astype(jnp.float32)
        hi = refb[2, hh * WROWS : hh * WROWS + 16, :].astype(jnp.float32)
        lo = jnp.where(tiles[1][band] >= 0, lo, 0.0)
        hi = jnp.where(tiles[2][band] >= 0, hi, 0.0)
        refx[hh, WROWS:PITCH, :] = jnp.where(edge == 0, hi, jnp.where(edge == 15, lo, 0.0))

    linef[...] = jnp.zeros_like(linef)
    vt0[...] = jnp.zeros_like(vt0)
    vte0[...] = jnp.zeros_like(vte0)

    def arrived(hh):
        pltpu.make_async_copy(lines.at[hh], lines.at[hh], sem_l.at[hh]).wait()

    lane40 = lax.broadcasted_iota(jnp.int32, (40, LANES), 1)

    def window(buf, first, rows, r0):
        shift = lax.rem(LANES - C * r0, LANES)
        a = pltpu.roll(buf[pl.ds(first, rows), :], shift, 1)
        b = pltpu.roll(buf[pl.ds(first + 1, rows), :], shift, 1)
        return jnp.where(lane40[:rows] < LANES - C * r0, a, b)

    def assemble(hh, carry):
        row = row_of(hh)
        for s in range(3):
            tt = tile_of(s, hh)
            total = None
            for u in range(NPV):
                off = tab[tt, 0, 2 * NPV * H + u * H + row]
                col = off + d0 - 2 + FRONT * COLS
                q = lax.div(col, COLS)
                r0 = col - q * COLS
                slot = s * NPV + u
                buf = linef.at[slot]
                buf[FRONT : FRONT + LROWS, :] = lines[hh, slot].astype(jnp.float32)
                if s == 0:
                    part = window(buf, q, 40, r0)
                elif s == 1:
                    part = window(buf, q + WROWS - 1, 8, r0)
                else:
                    part = window(buf, q, 8, r0)
                total = part if total is None else total + part
            if s == 0:
                vt0[hh, 0:40, :] = total
            else:
                vte0[s - 1, hh, 0:8, :] = total
        return carry

    lane1 = lax.broadcasted_iota(jnp.int32, (1, LANES), 1)

    lane_p = lax.broadcasted_iota(jnp.int32, (PITCH, LANES), 1)
    edge3 = lax.broadcasted_iota(jnp.int32, (16, LANES), 0) == 0
    lane_half = lax.rem(lane_p, LANES // 2)
    nk = (nd + 4) // COLS
    gm = group_matrix()

    def cost_row(hh, carry):
        for r in range(COLS):
            keep = lane1 < LANES - C * r

            def moved(x, y):
                if r == 0:
                    return x
                s = LANES - C * r
                return jnp.where(keep, pltpu.roll(x, s, 1), pltpu.roll(y, s, 1))

            vt[r] = moved(vt0[hh, 0:40, :], vt0[hh, 1:41, :])
            for side in range(2):
                vte[r, side] = moved(vte0[side, hh, 0:8, :], vte0[side, hh, 1:9, :])
        ref_rows = refx[hh]
        at = pl.multiple_of(hh * PITCH, 16)
        for k in range(nk):
            parts = []
            for r in range(COLS):
                own = vt[r, k : k + WROWS, :]
                side = jnp.where(edge3, vte[r, 1, k : k + 1, :], vte[r, 0, k : k + 1, :])
                prod = ref_rows * jnp.concatenate([own, side], axis=0)
                top = prod.astype(jnp.bfloat16)
                low = (prod - top.astype(jnp.float32)).astype(jnp.bfloat16)
                parts.append(jnp.concatenate([top, low], axis=1))
            cost = jnp.dot(jnp.concatenate(parts, axis=0), gm, preferred_element_type=jnp.float32)
            for r in range(COLS):
                c = cost[r * PITCH : (r + 1) * PITCH]
                x = jnp.where(
                    lane_half < COLS * G,
                    c,
                    jnp.where(lane_half < (COLS + 1) * G, pltpu.roll(c, 1, 0), pltpu.roll(c, PITCH - 1, 0)),
                )
                dd = k * COLS + r
                if dd < 2 or dd >= nd + 2:
                    disp = d0 - 2 + dd
                    x = jnp.where((disp >= 0) & (disp < NDISP), x, 0.0)
                both = jnp.where(lane_p < LANES // 2, xprev[dd], x)
                x1[dd, pl.ds(at, PITCH), :] = both.astype(jnp.bfloat16)
                xprev[dd] = x
        return carry

    arrived(0)
    assemble(0, 0)

    def row_fetching(hh, carry):
        arrived(hh + 1)
        fetch(hh + ahead, carry)
        cost_row(hh, carry)
        return assemble(hh + 1, carry)

    def row_only(hh, carry):
        arrived(hh + 1)
        cost_row(hh, carry)
        return assemble(hh + 1, carry)

    lax.fori_loop(0, HX - ahead, row_fetching, 0)
    lax.fori_loop(HX - ahead, HX - 1, row_only, 0)
    cost_row(HX - 1, 0)
    for dd in range(nk * COLS):
        x1[dd, HX * PITCH : (HX + 1) * PITCH, :] = xprev[dd].astype(jnp.bfloat16)

    rows1 = (H + 2) * PITCH
    row_id = lax.broadcasted_iota(jnp.int32, (rows1, LANES), 0)
    hrow = row_id // PITCH
    col = row_id - hrow * PITCH

    def inside(s):
        above = jnp.where(tiles[s][0] >= 0, 1, 0)
        mid = jnp.where(tiles[s][1] >= 0, 1, 0)
        below = jnp.where(tiles[s][2] >= 0, 1, 0)
        return jnp.where(hrow == 0, above, jnp.where(hrow == H + 1, below, mid))

    valid = jnp.where(col < WROWS, inside(0), jnp.where(col == WROWS, inside(2), inside(1)))
    bias1 = jnp.concatenate([b1[...]] * COLS, axis=1)
    bias2 = jnp.concatenate([b2[...]] * COLS, axis=1)
    lane_h = lax.broadcasted_iota(jnp.int32, (PITCH, LANES), 1)

    def layer1(d, carry):
        lhs = jnp.concatenate(
            [x1[d + a, b * PITCH : b * PITCH + rows1, :] for a in range(3) for b in (1, 3)], axis=1
        )
        y = jnp.dot(lhs, w1[...], preferred_element_type=jnp.float32)
        y = jnp.maximum(y + bias1, 0.0)
        disp = d0 - 1 + d
        least = jnp.where((disp >= 0) & (disp < NDISP), 0, 1)
        y = jnp.where(valid > least, y, 0.0)
        for hh in range(H + 2):
            z = y[hh * PITCH : (hh + 1) * PITCH]
            zr = pltpu.roll(z, C, 1)
            extra = jnp.where(lane_h < CH, pltpu.roll(zr, 1, 0), pltpu.roll(zr, PITCH - 1, 0))
            both = jnp.concatenate([z[:WROWS], extra[:WROWS]], axis=1)
            h2[d, hh * WROWS : (hh + 1) * WROWS, :] = both.astype(jnp.bfloat16)
        return carry

    rows2 = H * WROWS

    def layer2(d, slot):
        lhs = jnp.concatenate(
            [h2[d + a, b * WROWS : b * WROWS + rows2, :] for a in range(3) for b in range(3)], axis=1
        )
        y = ybuf.at[slot]
        y[...] = jnp.dot(lhs, w2[...], preferred_element_type=jnp.float32) + bias2
        for i in range(WROWS):
            out_ref[d, :, i * LANES : (i + 1) * LANES] = y[pl.ds(i, H, stride=WROWS), :]

    for d in range(4):
        layer1(d, 0)

    def both_layers(i, carry):
        layer2(2 * i, 0)
        layer2(2 * i + 1, 1)
        layer1(2 * i + 4, carry)
        layer1(2 * i + 5, carry)
        return carry

    lax.fori_loop(0, nd // 2 - 1, both_layers, 0)
    layer2(nd - 2, 0)
    layer2(nd - 1, 1)


def group_matrix():
    row = lax.broadcasted_iota(jnp.int32, (2 * LANES, LANES), 0)
    lane = lax.broadcasted_iota(jnp.int32, (2 * LANES, LANES), 1)
    source = lax.rem(row, LANES) // (C // G)
    lane = lax.rem(lane, LANES // 2)
    own = COLS * G
    target = jnp.where(
        lane < own, lane, jnp.where(lane < own + G, lane - G, jnp.where(lane < own + 2 * G, lane - own - G, -1))
    )
    return jnp.where(source == target, 1.0 / (NPV * (C // G)), 0.0).astype(jnp.bfloat16)


def on_device(
    ref_features, partner_lines, line_owner, line_index, line_offset, neighbours,
    conv1_weight, conv1_bias, conv2_weight, conv2_bias,
):
    n_tiles = lax.axis_size("tiles")
    views = lax.axis_size("views")
    nd = NDISP // views
    body = NPV * H * LROWS + H * WROWS
    total = -(-body // (32 * views)) * 32 * views
    vmem = pl.BlockSpec(memory_space=pltpu.VMEM)
    smem = pl.BlockSpec(memory_space=pltpu.SMEM)
    hbm = pl.BlockSpec(memory_space=pl.ANY)
    orders = hop_orders(n_tiles, views)
    dma = pltpu.SemaphoreType.DMA
    gathered, table, w1, w2 = pl.pallas_call(
        partial(gather_kernel, n_tiles, views),
        out_shape=[
            jax.ShapeDtypeStruct((n_tiles, total, LANES), jnp.bfloat16),
            jax.ShapeDtypeStruct((n_tiles, 8, LANES), jnp.int32),
            jax.ShapeDtypeStruct((6 * LANES, LANES), jnp.bfloat16),
            jax.ShapeDtypeStruct((18 * LANES, LANES), jnp.bfloat16),
        ],
        in_specs=[vmem] * 7,
        out_specs=[hbm, hbm, vmem, vmem],
        scratch_shapes=[
            pltpu.VMEM((total, LANES), jnp.float32),
            pltpu.VMEM((total // views, LANES), jnp.bfloat16),
            pltpu.VMEM((8, LANES), jnp.int32),
            dma((len(orders),)),
            *[dma((1 << len(order),)) for order in orders for _ in range(2)],
        ],
        compiler_params=pltpu.CompilerParams(
            collective_id=0, has_side_effects=True, vmem_limit_bytes=60 << 20
        ),
        name="gather",
    )(
        partner_lines[0].reshape(NPV * H, SW * C),
        ref_features[0],
        line_owner.reshape(1, NPV * H),
        line_index,
        line_offset,
        conv1_weight.reshape(27 * G, CH),
        conv2_weight.reshape(27 * CH, CH),
    )
    nk = (nd + 4) // COLS
    f32, bf16 = jnp.float32, jnp.bfloat16
    out = pl.pallas_call(
        partial(main_kernel, nd),
        out_shape=jax.ShapeDtypeStruct((nd, H, W * CH), f32),
        in_specs=[smem, hbm, hbm] + [vmem] * 4,
        out_specs=vmem,
        scratch_shapes=[
            pltpu.SMEM((n_tiles, 8, LANES), jnp.int32),
            pltpu.VMEM((HX, 3 * NPV, LROWS, LANES), bf16),
            pltpu.VMEM((3, HX * WROWS, LANES), bf16),
            pltpu.VMEM((3 * NPV, LPAD, LANES), f32),
            pltpu.VMEM((HX, 48, LANES), f32),
            pltpu.VMEM((2, HX, 16, LANES), f32),
            pltpu.VMEM((COLS, 40, LANES), f32),
            pltpu.VMEM((COLS, 2, 8, LANES), f32),
            pltpu.VMEM((HX, PITCH, LANES), f32),
            pltpu.VMEM((nk * COLS, PITCH, LANES), f32),
            pltpu.VMEM((nk * COLS, (HX + 1) * PITCH, LANES), bf16),
            pltpu.VMEM((nd + 2, (H + 2) * WROWS, 2 * LANES), bf16),
            pltpu.VMEM((2, H * WROWS, LANES), f32),
            dma((HX,)),
            dma((9,)),
            dma,
        ],
        compiler_params=pltpu.CompilerParams(vmem_limit_bytes=60 << 20),
        name="volume",
    )(
        neighbours.T,
        table,
        gathered,
        w1,
        conv1_bias[None],
        w2,
        conv2_bias[None],
    )
    return out[None]


def solution(mesh):
    return jax.shard_map(
        on_device,
        mesh=mesh,
        in_specs=(
            P("tiles", None, None),
            P("tiles", None, None, None),
            P("tiles", None, None),
            P("tiles", None),
            P("tiles", None),
            P(),
            P(),
            P(),
            P(),
            P(),
        ),
        out_specs=P("tiles", "views", None, None),
        check_vma=False,
    )
```

```python
import heapq
from functools import partial

import jax
import jax.numpy as jnp
from jax import lax
from jax.experimental import pallas as pl
from jax.experimental.pallas import tpu as pltpu
from jax.sharding import PartitionSpec as P

C = 32
G = 8
CH = 32
NDISP = 64
W = 128
SW = 256
NPV = 4
H = 8
LANES = 128
COLS = LANES // C
LROWS = SW // COLS
WROWS = W // COLS
PITCH = WROWS + 16
HX = H + 4
FRONT = 8
LPAD = FRONT + LROWS + 8
MESH = pl.DeviceIdType.MESH


def spread_taps(raw_ref, out_ref, depth, pitch):
    k = raw_ref.shape[0] // 27
    group = lax.broadcasted_iota(jnp.int32, (k, LANES), 1) // CH
    for ab in range(9):
        taps = []
        for e in range(3):
            at = (ab * 3 + e) * k
            tap = raw_ref[at : at + k, :].astype(jnp.float32)
            taps.append(jnp.concatenate([tap] * COLS, axis=1))
        rows = []
        for c in list(range(COLS)) + [-1, COLS]:
            row = jnp.zeros((k, LANES), jnp.float32)
            for e in range(3):
                row = jnp.where(group == c + 1 - e, taps[e], row)
            rows.append(row)
        rows.append(jnp.zeros((depth - len(rows) * k, LANES), jnp.float32))
        at = ab // 3 * pitch + ab % 3 * depth
        out_ref[at : at + depth, :] = jnp.concatenate(rows, axis=0).astype(jnp.bfloat16)
    if pitch > 3 * depth:
        for a in range(3):
            out_ref[a * pitch + 3 * depth : (a + 1) * pitch, :] = jnp.zeros((pitch - 3 * depth, LANES), jnp.bfloat16)


def pack_own(lines_ref, ref_ref, scr, part_ref):
    n_lines = lines_ref.shape[0]
    for j in range(LROWS):
        scr[pl.ds(j, n_lines, stride=LROWS), :] = lines_ref[:, j * LANES : (j + 1) * LANES].astype(jnp.float32)
    base = n_lines * LROWS
    for i in range(WROWS):
        scr[pl.ds(base + i, H, stride=WROWS), :] = ref_ref[:, i * LANES : (i + 1) * LANES].astype(jnp.float32)
    base = base + H * WROWS
    if scr.shape[0] > base:
        scr[base:, :] = jnp.zeros((scr.shape[0] - base, LANES), jnp.float32)
    part_ref[...] = scr[...].astype(jnp.bfloat16)


def hop_orders(T, V):
    def bits(axis, size):
        out = []
        while size > 1:
            size //= 2
            out.append((axis, size))
        return out

    tb, vb = bits(0, T), bits(1, V)
    first = tb + vb
    second = tb[:-1] + vb[:1] + tb[-1:] + vb[1:]
    third = tb[:1] + tb[-1:] + vb[:1] + tb[1:-1] + vb[1:]
    return first, second, third, tb


def split_rows(part):
    units = part // 16
    third = units // 4
    second = (units - third) * 2 // 5
    return [(units - second - third) * 16, second * 16, third * 16]


def own_masks(order):
    views = [1 << h for h, (axis, _) in enumerate(order) if axis == 1]
    masks = [0]
    for bit in views:
        masks = masks + [mask | bit for mask in masks]
    return masks


def arrivals(orders, costs):
    free = {}
    heap = []
    for o, order in enumerate(orders):
        for mask in own_masks(order):
            heapq.heappush(heap, (0.0, o, mask))
    seen = []
    while heap:
        now, o, mask = heapq.heappop(heap)
        seen.append((o, mask))
        for h in onward(orders[o], mask):
            axis, bit = orders[o][h]
            link = (axis, min(bit, 2))
            free[link] = max(free.get(link, 0.0), now) + costs[o] * (0.2 if link == (1, 1) else 1.0)
            heapq.heappush(heap, (free[link] + 0.5, o, mask | (1 << h)))
    return seen


def onward(order, mask):
    own = own_masks(order)
    return [h for h in range(mask.bit_length(), len(order)) if mask | (1 << h) not in own]


def gather_kernel(
    T, V, lines_ref, ref_ref, owner_ref, index_ref, offset_ref, k1_ref, k2_ref,
    all_ref, tab_ref, w1_ref, w2_ref, scr, part_ref, req_ref, own_sem, *sems
):
    t = lax.axis_index("tiles")
    v = lax.axis_index("views")
    part = part_ref.shape[0] // V
    orders = hop_orders(T, V)
    counts = split_rows(part)
    starts = [sum(counts[:o]) for o in range(len(counts))]
    last = len(orders) - 1

    def flip(x, bit):
        return x + bit - 2 * bit * lax.rem(lax.div(x, bit), 2)

    def across(mask, order):
        at = [t, v]
        for h, (axis, bit) in enumerate(order):
            if mask >> h & 1:
                at[axis] = flip(at[axis], bit)
        return tuple(at)

    barrier = pltpu.get_barrier_semaphore()
    hops = orders[0]
    for hop in hops:
        pl.semaphore_signal(barrier, inc=1, device_id=across(1, [hop]), device_id_type=MESH)
    pack_own(lines_ref, ref_ref, scr, part_ref)
    asked = [owner_ref[...], index_ref[...], offset_ref[...]]
    asked.append(jnp.zeros((1, LANES - 3 * asked[0].shape[1]), jnp.int32))
    req_ref[...] = jnp.broadcast_to(jnp.concatenate(asked, axis=1), req_ref.shape)
    pl.semaphore_wait(barrier, len(hops))

    def place(o, mask):
        tile, view = across(mask, orders[o])
        if o == last:
            return tab_ref.at[tile]
        return all_ref.at[tile, pl.ds(pl.multiple_of(view * part + starts[o], 16), counts[o]), :]

    def source(o, mask):
        if mask not in own_masks(orders[o]):
            return place(o, mask)
        if o == last:
            return req_ref
        view = across(mask, orders[o])[1]
        return part_ref.at[pl.ds(pl.multiple_of(view * part + starts[o], 16), counts[o]), :]

    def send(o, mask, h):
        return pltpu.make_async_remote_copy(
            src_ref=source(o, mask),
            dst_ref=place(o, mask),
            send_sem=sems[2 * o].at[mask | (1 << h)],
            recv_sem=sems[2 * o + 1].at[mask | (1 << h)],
            device_id=across(1 << h, orders[o]),
            device_id_type=MESH,
        )

    def landed(o, mask):
        return pltpu.make_async_remote_copy(
            src_ref=place(o, mask),
            dst_ref=place(o, mask),
            send_sem=sems[2 * o].at[mask],
            recv_sem=sems[2 * o + 1].at[mask],
            device_id=across(1, orders[o]),
            device_id_type=MESH,
        )

    own = [
        pltpu.make_async_copy(part_ref, all_ref.at[t], own_sem.at[0]),
        pltpu.make_async_copy(req_ref, tab_ref.at[t], own_sem.at[1]),
    ]
    sent = []
    scale = 1.0 / part
    landing = arrivals(orders, [count * scale for count in counts] + [0.01])
    for n, (o, mask) in enumerate(landing):
        if n == len(landing) // 2:
            for copy in own:
                copy.start()
            spread_taps(k1_ref, w1_ref, LANES // 2, 2 * LANES)
            spread_taps(k2_ref, w2_ref, 2 * LANES, 6 * LANES)
        if mask not in own_masks(orders[o]):
            landed(o, mask).wait_recv()
        for h in onward(orders[o], mask):
            copy = send(o, mask, h)
            copy.start()
            sent.append(copy)
    for copy in own:
        copy.wait()
    for copy in sent:
        copy.wait_send()


def main_kernel(
    nd, nb, tab_ref, all_ref, w1_ref, b1, w2_ref, b2, out_ref,
    w1, w2, obuf, tab, lines, refb, linef, vt0, vte0, vt, vte, refx, xprev, x1, h2, ybuf, sem_l, sem_r, sem_t, sem_w, sem_o,
):
    table_copy = pltpu.make_async_copy(tab_ref, tab, sem_t)
    table_copy.start()
    weights = [
        pltpu.make_async_copy(w1_ref, w1, sem_w.at[0]),
        pltpu.make_async_copy(w2_ref, w2, sem_w.at[1]),
    ]
    t = lax.axis_index("tiles")
    v = lax.axis_index("views")
    d0 = v * nd

    def link(x, side):
        got = nb[side, jnp.maximum(x, 0)]
        return jnp.where(x >= 0, got, -1)

    mids = [t, link(t, 2), link(t, 3)]
    tiles = [[link(m, 0), m, link(m, 1)] for m in mids]
    ref_base = NPV * H * LROWS

    spans = ((0, 2, H - 2), (2, H, 0), (H + 2, 2, 0))
    copies = []
    for s in range(3):
        for band, (at, count, row) in enumerate(spans):
            copies.append(
                pltpu.make_async_copy(
                    all_ref.at[jnp.maximum(tiles[s][band], 0), pl.ds(ref_base + row * WROWS, count * WROWS), :],
                    refb.at[s, pl.ds(at * WROWS, count * WROWS), :],
                    sem_r.at[s * 3 + band],
                )
            )
    for c in copies:
        c.start()

    def tile_of(s, hh):
        return jnp.maximum(
            jnp.where(hh < 2, tiles[s][0], jnp.where(hh < H + 2, tiles[s][1], tiles[s][2])), 0
        )

    def row_of(hh):
        return jnp.where(hh < 2, hh + H - 2, jnp.where(hh < H + 2, hh - 2, hh - H - 2))

    table_copy.wait()

    def fetch(hh, carry):
        row = row_of(hh)
        for s in range(3):
            tt = tile_of(s, hh)
            for u in range(NPV):
                owner = tab[tt, 0, u * H + row]
                index = tab[tt, 0, NPV * H + u * H + row]
                src = pl.multiple_of((u * H + index) * LROWS, LROWS)
                pltpu.make_async_copy(
                    all_ref.at[owner, pl.ds(src, LROWS), :], lines.at[hh, s * NPV + u], sem_l.at[hh]
                ).start()
        return carry

    ahead = 4
    lax.fori_loop(0, ahead, fetch, 0)
    for copy in weights:
        copy.start()

    for c in copies:
        c.wait()
    edge = lax.broadcasted_iota(jnp.int32, (16, LANES), 0)
    for hh in range(HX):
        band = 0 if hh < 2 else (1 if hh < H + 2 else 2)
        own = refb[0, hh * WROWS : (hh + 1) * WROWS, :].astype(jnp.float32)
        refx[hh, 0:WROWS, :] = jnp.where(tiles[0][band] >= 0, own, 0.0)
        lo = refb[1, (hh + 1) * WROWS - 16 : (hh + 1) * WROWS, :].astype(jnp.float32)
        hi = refb[2, hh * WROWS : hh * WROWS + 16, :].astype(jnp.float32)
        lo = jnp.where(tiles[1][band] >= 0, lo, 0.0)
        hi = jnp.where(tiles[2][band] >= 0, hi, 0.0)
        refx[hh, WROWS:PITCH, :] = jnp.where(edge == 0, hi, jnp.where(edge == 15, lo, 0.0))

    linef[...] = jnp.zeros_like(linef)
    vt0[...] = jnp.zeros_like(vt0)
    vte0[...] = jnp.zeros_like(vte0)

    def arrived(hh):
        pltpu.make_async_copy(lines.at[hh], lines.at[hh], sem_l.at[hh]).wait()

    lane40 = lax.broadcasted_iota(jnp.int32, (40, LANES), 1)

    def window(buf, first, rows, r0):
        shift = lax.rem(LANES - C * r0, LANES)
        a = pltpu.roll(buf[pl.ds(first, rows), :], shift, 1)
        b = pltpu.roll(buf[pl.ds(first + 1, rows), :], shift, 1)
        return jnp.where(lane40[:rows] < LANES - C * r0, a, b)

    def assemble(hh, carry):
        row = row_of(hh)
        for s in range(3):
            tt = tile_of(s, hh)
            total = None
            for u in range(NPV):
                off = tab[tt, 0, 2 * NPV * H + u * H + row]
                col = off + d0 - 2 + FRONT * COLS
                q = lax.div(col, COLS)
                r0 = col - q * COLS
                slot = s * NPV + u
                buf = linef.at[slot]
                buf[FRONT : FRONT + LROWS, :] = lines[hh, slot].astype(jnp.float32)
                if s == 0:
                    part = window(buf, q, 40, r0)
                elif s == 1:
                    part = window(buf, q + WROWS - 1, 8, r0)
                else:
                    part = window(buf, q, 8, r0)
                total = part if total is None else total + part
            if s == 0:
                vt0[hh, 0:40, :] = total
            else:
                vte0[s - 1, hh, 0:8, :] = total
        return carry

    lane1 = lax.broadcasted_iota(jnp.int32, (1, LANES), 1)

    lane_p = lax.broadcasted_iota(jnp.int32, (PITCH, LANES), 1)
    edge3 = lax.broadcasted_iota(jnp.int32, (16, LANES), 0) == 0
    lane_half = lax.rem(lane_p, LANES // 2)
    nk = (nd + 4) // COLS
    gm = group_matrix()

    def cost_row(hh, carry):
        for r in range(COLS):
            keep = lane1 < LANES - C * r

            def moved(x, y):
                if r == 0:
                    return x
                s = LANES - C * r
                return jnp.where(keep, pltpu.roll(x, s, 1), pltpu.roll(y, s, 1))

            vt[r] = moved(vt0[hh, 0:40, :], vt0[hh, 1:41, :])
            for side in range(2):
                vte[r, side] = moved(vte0[side, hh, 0:8, :], vte0[side, hh, 1:9, :])
        ref_rows = refx[hh]
        at = pl.multiple_of(hh * PITCH, 16)
        for k in range(nk):
            parts = []
            for r in range(COLS):
                own = vt[r, k : k + WROWS, :]
                side = jnp.where(edge3, vte[r, 1, k : k + 1, :], vte[r, 0, k : k + 1, :])
                prod = ref_rows * jnp.concatenate([own, side], axis=0)
                top = prod.astype(jnp.bfloat16)
                low = (prod - top.astype(jnp.float32)).astype(jnp.bfloat16)
                parts.append(jnp.concatenate([top, low], axis=1))
            cost = jnp.dot(jnp.concatenate(parts, axis=0), gm, preferred_element_type=jnp.float32)
            for r in range(COLS):
                c = cost[r * PITCH : (r + 1) * PITCH]
                x = jnp.where(
                    lane_half < COLS * G,
                    c,
                    jnp.where(lane_half < (COLS + 1) * G, pltpu.roll(c, 1, 0), pltpu.roll(c, PITCH - 1, 0)),
                )
                dd = k * COLS + r
                if dd < 2 or dd >= nd + 2:
                    disp = d0 - 2 + dd
                    x = jnp.where((disp >= 0) & (disp < NDISP), x, 0.0)
                both = jnp.where(lane_p < LANES // 2, xprev[dd], x)
                x1[dd, pl.ds(at, PITCH), :] = both.astype(jnp.bfloat16)
                xprev[dd] = x
        return carry

    arrived(0)
    assemble(0, 0)

    def row_fetching(hh, carry):
        arrived(hh + 1)
        fetch(hh + ahead, carry)
        cost_row(hh, carry)
        return assemble(hh + 1, carry)

    def row_only(hh, carry):
        arrived(hh + 1)
        cost_row(hh, carry)
        return assemble(hh + 1, carry)

    lax.fori_loop(0, HX - ahead, row_fetching, 0)
    lax.fori_loop(HX - ahead, HX - 1, row_only, 0)
    cost_row(HX - 1, 0)
    for dd in range(nk * COLS):
        x1[dd, HX * PITCH : (HX + 1) * PITCH, :] = xprev[dd].astype(jnp.bfloat16)

    rows1 = (H + 2) * PITCH
    row_id = lax.broadcasted_iota(jnp.int32, (rows1, LANES), 0)
    hrow = row_id // PITCH
    col = row_id - hrow * PITCH

    def inside(s):
        above = jnp.where(tiles[s][0] >= 0, 1, 0)
        mid = jnp.where(tiles[s][1] >= 0, 1, 0)
        below = jnp.where(tiles[s][2] >= 0, 1, 0)
        return jnp.where(hrow == 0, above, jnp.where(hrow == H + 1, below, mid))

    valid = jnp.where(col < WROWS, inside(0), jnp.where(col == WROWS, inside(2), inside(1)))
    bias1 = jnp.concatenate([b1[...]] * COLS, axis=1)
    bias2 = jnp.concatenate([b2[...]] * COLS, axis=1)
    lane_h = lax.broadcasted_iota(jnp.int32, (PITCH, LANES), 1)

    def layer1(d, carry):
        lhs = jnp.concatenate(
            [x1[d + a, b * PITCH : b * PITCH + rows1, :] for a in range(3) for b in (1, 3)], axis=1
        )
        y = jnp.dot(lhs, w1[...], preferred_element_type=jnp.float32)
        y = jnp.maximum(y + bias1, 0.0)
        disp = d0 - 1 + d
        least = jnp.where((disp >= 0) & (disp < NDISP), 0, 1)
        y = jnp.where(valid > least, y, 0.0)
        for hh in range(H + 2):
            z = y[hh * PITCH : (hh + 1) * PITCH]
            zr = pltpu.roll(z, C, 1)
            extra = jnp.where(lane_h < CH, pltpu.roll(zr, 1, 0), pltpu.roll(zr, PITCH - 1, 0))
            both = jnp.concatenate([z[:WROWS], extra[:WROWS]], axis=1)
            h2[d, hh * WROWS : (hh + 1) * WROWS, :] = both.astype(jnp.bfloat16)
        return carry

    rows2 = H * WROWS

    def slab_out(d):
        return pltpu.make_async_copy(obuf.at[d], out_ref.at[d], sem_o.at[d])

    def layer2(d, slot):
        lhs = jnp.concatenate(
            [h2[d + a, b * WROWS : b * WROWS + rows2, :] for a in range(3) for b in range(3)], axis=1
        )
        y = ybuf.at[slot]
        y[...] = jnp.dot(lhs, w2[...], preferred_element_type=jnp.float32) + bias2
        for i in range(WROWS):
            obuf[d, :, i * LANES : (i + 1) * LANES] = y[pl.ds(i, H, stride=WROWS), :]
        slab_out(d).start()

    for copy in weights:
        copy.wait()
    for d in range(4):
        layer1(d, 0)

    def both_layers(i, carry):
        layer2(2 * i, 0)
        layer2(2 * i + 1, 1)
        layer1(2 * i + 4, carry)
        layer1(2 * i + 5, carry)
        return carry

    lax.fori_loop(0, nd // 2 - 1, both_layers, 0)
    layer2(nd - 2, 0)
    layer2(nd - 1, 1)

    def slab_done(d, carry):
        slab_out(d).wait()
        return carry

    lax.fori_loop(0, nd, slab_done, 0)


def group_matrix():
    row = lax.broadcasted_iota(jnp.int32, (2 * LANES, LANES), 0)
    lane = lax.broadcasted_iota(jnp.int32, (2 * LANES, LANES), 1)
    source = lax.rem(row, LANES) // (C // G)
    lane = lax.rem(lane, LANES // 2)
    own = COLS * G
    target = jnp.where(
        lane < own, lane, jnp.where(lane < own + G, lane - G, jnp.where(lane < own + 2 * G, lane - own - G, -1))
    )
    return jnp.where(source == target, 1.0 / (NPV * (C // G)), 0.0).astype(jnp.bfloat16)


def on_device(
    ref_features, partner_lines, line_owner, line_index, line_offset, neighbours,
    conv1_weight, conv1_bias, conv2_weight, conv2_bias,
):
    n_tiles = lax.axis_size("tiles")
    views = lax.axis_size("views")
    nd = NDISP // views
    body = NPV * H * LROWS + H * WROWS
    total = -(-body // (16 * views)) * 16 * views
    vmem = pl.BlockSpec(memory_space=pltpu.VMEM)
    smem = pl.BlockSpec(memory_space=pltpu.SMEM)
    hbm = pl.BlockSpec(memory_space=pl.ANY)
    orders = hop_orders(n_tiles, views)
    dma = pltpu.SemaphoreType.DMA
    gathered, table, w1, w2 = pl.pallas_call(
        partial(gather_kernel, n_tiles, views),
        out_shape=[
            jax.ShapeDtypeStruct((n_tiles, total, LANES), jnp.bfloat16),
            jax.ShapeDtypeStruct((n_tiles, 8, LANES), jnp.int32),
            jax.ShapeDtypeStruct((6 * LANES, LANES), jnp.bfloat16),
            jax.ShapeDtypeStruct((18 * LANES, LANES), jnp.bfloat16),
        ],
        in_specs=[vmem] * 7,
        out_specs=[hbm, hbm, vmem, vmem],
        scratch_shapes=[
            pltpu.VMEM((total, LANES), jnp.float32),
            pltpu.VMEM((total, LANES), jnp.bfloat16),
            pltpu.VMEM((8, LANES), jnp.int32),
            dma((2,)),
            *[dma((1 << len(order),)) for order in orders for _ in range(2)],
        ],
        compiler_params=pltpu.CompilerParams(
            collective_id=0, has_side_effects=True, vmem_limit_bytes=60 << 20
        ),
        name="gather",
    )(
        partner_lines[0].reshape(NPV * H, SW * C),
        ref_features[0],
        line_owner.reshape(1, NPV * H),
        line_index,
        line_offset,
        conv1_weight.reshape(27 * G, CH),
        conv2_weight.reshape(27 * CH, CH),
    )
    nk = (nd + 4) // COLS
    f32, bf16 = jnp.float32, jnp.bfloat16
    out = pl.pallas_call(
        partial(main_kernel, nd),
        out_shape=jax.ShapeDtypeStruct((nd, H, W * CH), f32),
        in_specs=[smem, hbm, hbm, hbm, vmem, hbm, vmem],
        out_specs=hbm,
        scratch_shapes=[
            pltpu.VMEM((6 * LANES, LANES), bf16),
            pltpu.VMEM((18 * LANES, LANES), bf16),
            pltpu.VMEM((nd, H, W * CH), f32),
            pltpu.SMEM((n_tiles, 8, LANES), jnp.int32),
            pltpu.VMEM((HX, 3 * NPV, LROWS, LANES), bf16),
            pltpu.VMEM((3, HX * WROWS, LANES), bf16),
            pltpu.VMEM((3 * NPV, LPAD, LANES), f32),
            pltpu.VMEM((HX, 48, LANES), f32),
            pltpu.VMEM((2, HX, 16, LANES), f32),
            pltpu.VMEM((COLS, 40, LANES), f32),
            pltpu.VMEM((COLS, 2, 8, LANES), f32),
            pltpu.VMEM((HX, PITCH, LANES), f32),
            pltpu.VMEM((nk * COLS, PITCH, LANES), f32),
            pltpu.VMEM((nk * COLS, (HX + 1) * PITCH, LANES), bf16),
            pltpu.VMEM((nd + 2, (H + 2) * WROWS, 2 * LANES), bf16),
            pltpu.VMEM((2, H * WROWS, LANES), f32),
            dma((HX,)),
            dma((9,)),
            dma,
            dma((2,)),
            dma((nd,)),
        ],
        compiler_params=pltpu.CompilerParams(vmem_limit_bytes=60 << 20),
        name="volume",
    )(
        neighbours.T,
        table,
        gathered,
        w1,
        conv1_bias[None],
        w2,
        conv2_bias[None],
    )
    return out[None]


def solution(mesh):
    return jax.shard_map(
        on_device,
        mesh=mesh,
        in_specs=(
            P("tiles", None, None),
            P("tiles", None, None, None),
            P("tiles", None, None),
            P("tiles", None),
            P("tiles", None),
            P(),
            P(),
            P(),
            P(),
            P(),
        ),
        out_specs=P("tiles", "views", None, None),
        check_vma=False,
    )
```

```python
import heapq
from functools import partial

import jax
import jax.numpy as jnp
from jax import lax
from jax.experimental import pallas as pl
from jax.experimental.pallas import tpu as pltpu
from jax.sharding import PartitionSpec as P

C = 32
G = 8
CH = 32
NDISP = 64
W = 128
SW = 256
NPV = 4
H = 8
LANES = 128
COLS = LANES // C
LROWS = SW // COLS
WROWS = W // COLS
PITCH = WROWS + 16
HX = H + 4
FRONT = 8
LPAD = FRONT + LROWS + 8
MESH = pl.DeviceIdType.MESH


def spread_taps(raw_ref, out_ref, depth, pitch):
    k = raw_ref.shape[0] // 27
    group = lax.broadcasted_iota(jnp.int32, (k, LANES), 1) // CH
    for ab in range(9):
        taps = []
        for e in range(3):
            at = (ab * 3 + e) * k
            tap = raw_ref[at : at + k, :].astype(jnp.float32)
            taps.append(jnp.concatenate([tap] * COLS, axis=1))
        rows = []
        for c in list(range(COLS)) + [-1, COLS]:
            row = jnp.zeros((k, LANES), jnp.float32)
            for e in range(3):
                row = jnp.where(group == c + 1 - e, taps[e], row)
            rows.append(row)
        rows.append(jnp.zeros((depth - len(rows) * k, LANES), jnp.float32))
        at = ab // 3 * pitch + ab % 3 * depth
        out_ref[at : at + depth, :] = jnp.concatenate(rows, axis=0).astype(jnp.bfloat16)
    if pitch > 3 * depth:
        for a in range(3):
            out_ref[a * pitch + 3 * depth : (a + 1) * pitch, :] = jnp.zeros((pitch - 3 * depth, LANES), jnp.bfloat16)


def pack_own(lines_ref, ref_ref, scr, part_ref):
    n_lines = lines_ref.shape[0]
    for j in range(LROWS):
        scr[pl.ds(j, n_lines, stride=LROWS), :] = lines_ref[:, j * LANES : (j + 1) * LANES].astype(jnp.float32)
    base = n_lines * LROWS
    for i in range(WROWS):
        scr[pl.ds(base + i, H, stride=WROWS), :] = ref_ref[:, i * LANES : (i + 1) * LANES].astype(jnp.float32)
    base = base + H * WROWS
    if scr.shape[0] > base:
        scr[base:, :] = jnp.zeros((scr.shape[0] - base, LANES), jnp.float32)
    part_ref[...] = scr[...].astype(jnp.bfloat16)


def hop_orders(T, V):
    def bits(axis, size):
        out = []
        while size > 1:
            size //= 2
            out.append((axis, size))
        return out

    tb, vb = bits(0, T), bits(1, V)
    first = tb + vb
    second = tb[:-1] + vb[:1] + tb[-1:] + vb[1:]
    third = tb[:1] + tb[-1:] + vb[:1] + tb[1:-1] + vb[1:]
    return first, second, third, tb


def split_rows(part):
    units = part // 16
    third = units // 4
    second = (units - third) * 2 // 5
    return [(units - second - third) * 16, second * 16, third * 16]


def own_masks(order):
    views = [1 << h for h, (axis, _) in enumerate(order) if axis == 1]
    masks = [0]
    for bit in views:
        masks = masks + [mask | bit for mask in masks]
    return masks


def arrivals(orders, costs):
    free = {}
    heap = []
    for o, order in enumerate(orders):
        for mask in own_masks(order):
            heapq.heappush(heap, (0.0, o, mask))
    seen = []
    while heap:
        now, o, mask = heapq.heappop(heap)
        seen.append((o, mask))
        for h in onward(orders[o], mask):
            axis, bit = orders[o][h]
            link = (axis, min(bit, 2))
            free[link] = max(free.get(link, 0.0), now) + costs[o] * (0.2 if link == (1, 1) else 1.0)
            heapq.heappush(heap, (free[link] + 0.5, o, mask | (1 << h)))
    return seen


def onward(order, mask):
    own = own_masks(order)
    return [h for h in range(mask.bit_length(), len(order)) if mask | (1 << h) not in own]


def gather_kernel(
    T, V, lines_ref, ref_ref, owner_ref, index_ref, offset_ref, k1_ref, k2_ref,
    all_ref, tab_ref, w1_ref, w2_ref, scr, part_ref, req_ref, own_sem, *sems
):
    t = lax.axis_index("tiles")
    v = lax.axis_index("views")
    part = part_ref.shape[0] // V
    orders = hop_orders(T, V)
    counts = split_rows(part)
    starts = [sum(counts[:o]) for o in range(len(counts))]
    last = len(orders) - 1

    def flip(x, bit):
        return x + bit - 2 * bit * lax.rem(lax.div(x, bit), 2)

    def across(mask, order):
        at = [t, v]
        for h, (axis, bit) in enumerate(order):
            if mask >> h & 1:
                at[axis] = flip(at[axis], bit)
        return tuple(at)

    barrier = pltpu.get_barrier_semaphore()
    hops = orders[0]
    for hop in hops:
        pl.semaphore_signal(barrier, inc=1, device_id=across(1, [hop]), device_id_type=MESH)
    pack_own(lines_ref, ref_ref, scr, part_ref)
    asked = [owner_ref[...], index_ref[...], offset_ref[...]]
    asked.append(jnp.zeros((1, LANES - 3 * asked[0].shape[1]), jnp.int32))
    req_ref[...] = jnp.broadcast_to(jnp.concatenate(asked, axis=1), req_ref.shape)
    pl.semaphore_wait(barrier, len(hops))

    def place(o, mask):
        tile, view = across(mask, orders[o])
        if o == last:
            return tab_ref.at[tile]
        return all_ref.at[tile, pl.ds(pl.multiple_of(view * part + starts[o], 16), counts[o]), :]

    def source(o, mask):
        if mask not in own_masks(orders[o]):
            return place(o, mask)
        if o == last:
            return req_ref
        view = across(mask, orders[o])[1]
        return part_ref.at[pl.ds(pl.multiple_of(view * part + starts[o], 16), counts[o]), :]

    def send(o, mask, h):
        return pltpu.make_async_remote_copy(
            src_ref=source(o, mask),
            dst_ref=place(o, mask),
            send_sem=sems[2 * o].at[mask | (1 << h)],
            recv_sem=sems[2 * o + 1].at[mask | (1 << h)],
            device_id=across(1 << h, orders[o]),
            device_id_type=MESH,
        )

    def landed(o, mask):
        return pltpu.make_async_remote_copy(
            src_ref=place(o, mask),
            dst_ref=place(o, mask),
            send_sem=sems[2 * o].at[mask],
            recv_sem=sems[2 * o + 1].at[mask],
            device_id=across(1, orders[o]),
            device_id_type=MESH,
        )

    own = [
        pltpu.make_async_copy(part_ref, all_ref.at[t], own_sem.at[0]),
        pltpu.make_async_copy(req_ref, tab_ref.at[t], own_sem.at[1]),
    ]
    sent = []
    scale = 1.0 / part
    landing = arrivals(orders, [count * scale for count in counts] + [0.01])
    for n, (o, mask) in enumerate(landing):
        if n == len(landing) // 2:
            for copy in own:
                copy.start()
            spread_taps(k1_ref, w1_ref, LANES // 2, 2 * LANES)
            spread_taps(k2_ref, w2_ref, 2 * LANES, 6 * LANES)
        if mask not in own_masks(orders[o]):
            landed(o, mask).wait_recv()
        for h in onward(orders[o], mask):
            copy = send(o, mask, h)
            copy.start()
            sent.append(copy)
    for copy in own:
        copy.wait()
    for copy in sent:
        copy.wait_send()


def main_kernel(
    nd, nb, tab_ref, all_ref, w1_ref, b1, w2_ref, b2, out_ref,
    w1, w2, obuf, tab, lines, refb, linef, vt0, vte0, vt, vte, refx, xprev, x1, h2, ybuf, sem_l, sem_r, sem_t, sem_w, sem_o,
):
    table_copy = pltpu.make_async_copy(tab_ref, tab, sem_t)
    table_copy.start()
    weights = []
    for n, (src, dst) in enumerate(((w1_ref, w1), (w2_ref, w2))):
        depth = src.shape[0]
        tap = depth // 3
        weights.append(pltpu.make_async_copy(src, dst.at[0:depth, 0:LANES], sem_w.at[2 * n]))
        weights.append(
            pltpu.make_async_copy(src, dst.at[tap : tap + depth, LANES : 2 * LANES], sem_w.at[2 * n + 1])
        )
        dst[depth:, 0:LANES] = jnp.zeros((tap, LANES), jnp.bfloat16)
        dst[0:tap, LANES : 2 * LANES] = jnp.zeros((tap, LANES), jnp.bfloat16)
    t = lax.axis_index("tiles")
    v = lax.axis_index("views")
    d0 = v * nd

    def link(x, side):
        got = nb[side, jnp.maximum(x, 0)]
        return jnp.where(x >= 0, got, -1)

    mids = [t, link(t, 2), link(t, 3)]
    tiles = [[link(m, 0), m, link(m, 1)] for m in mids]
    ref_base = NPV * H * LROWS

    spans = ((0, 2, H - 2), (2, H, 0), (H + 2, 2, 0))
    copies = []
    for s in range(3):
        for band, (at, count, row) in enumerate(spans):
            copies.append(
                pltpu.make_async_copy(
                    all_ref.at[jnp.maximum(tiles[s][band], 0), pl.ds(ref_base + row * WROWS, count * WROWS), :],
                    refb.at[s, pl.ds(at * WROWS, count * WROWS), :],
                    sem_r.at[s * 3 + band],
                )
            )
    for c in copies:
        c.start()

    def tile_of(s, hh):
        return jnp.maximum(
            jnp.where(hh < 2, tiles[s][0], jnp.where(hh < H + 2, tiles[s][1], tiles[s][2])), 0
        )

    def row_of(hh):
        return jnp.where(hh < 2, hh + H - 2, jnp.where(hh < H + 2, hh - 2, hh - H - 2))

    table_copy.wait()

    def fetch(hh, carry):
        row = row_of(hh)
        for s in range(3):
            tt = tile_of(s, hh)
            for u in range(NPV):
                owner = tab[tt, 0, u * H + row]
                index = tab[tt, 0, NPV * H + u * H + row]
                src = pl.multiple_of((u * H + index) * LROWS, LROWS)
                pltpu.make_async_copy(
                    all_ref.at[owner, pl.ds(src, LROWS), :], lines.at[hh, s * NPV + u], sem_l.at[hh]
                ).start()
        return carry

    ahead = 4
    lax.fori_loop(0, ahead, fetch, 0)
    for copy in weights:
        copy.start()

    for c in copies:
        c.wait()
    edge = lax.broadcasted_iota(jnp.int32, (16, LANES), 0)
    for hh in range(HX):
        band = 0 if hh < 2 else (1 if hh < H + 2 else 2)
        own = refb[0, hh * WROWS : (hh + 1) * WROWS, :].astype(jnp.float32)
        refx[hh, 0:WROWS, :] = jnp.where(tiles[0][band] >= 0, own, 0.0)
        lo = refb[1, (hh + 1) * WROWS - 16 : (hh + 1) * WROWS, :].astype(jnp.float32)
        hi = refb[2, hh * WROWS : hh * WROWS + 16, :].astype(jnp.float32)
        lo = jnp.where(tiles[1][band] >= 0, lo, 0.0)
        hi = jnp.where(tiles[2][band] >= 0, hi, 0.0)
        refx[hh, WROWS:PITCH, :] = jnp.where(edge == 0, hi, jnp.where(edge == 15, lo, 0.0))

    linef[...] = jnp.zeros_like(linef)
    vt0[...] = jnp.zeros_like(vt0)
    vte0[...] = jnp.zeros_like(vte0)

    def arrived(hh):
        pltpu.make_async_copy(lines.at[hh], lines.at[hh], sem_l.at[hh]).wait()

    lane40 = lax.broadcasted_iota(jnp.int32, (40, LANES), 1)

    def window(buf, first, rows, r0):
        shift = lax.rem(LANES - C * r0, LANES)
        a = pltpu.roll(buf[pl.ds(first, rows), :], shift, 1)
        b = pltpu.roll(buf[pl.ds(first + 1, rows), :], shift, 1)
        return jnp.where(lane40[:rows] < LANES - C * r0, a, b)

    def assemble(hh, carry):
        row = row_of(hh)
        for s in range(3):
            tt = tile_of(s, hh)
            total = None
            for u in range(NPV):
                off = tab[tt, 0, 2 * NPV * H + u * H + row]
                col = off + d0 - 2 + FRONT * COLS
                q = lax.div(col, COLS)
                r0 = col - q * COLS
                slot = s * NPV + u
                buf = linef.at[slot]
                buf[FRONT : FRONT + LROWS, :] = lines[hh, slot].astype(jnp.float32)
                if s == 0:
                    part = window(buf, q, 40, r0)
                elif s == 1:
                    part = window(buf, q + WROWS - 1, 8, r0)
                else:
                    part = window(buf, q, 8, r0)
                total = part if total is None else total + part
            if s == 0:
                vt0[hh, 0:40, :] = total
            else:
                vte0[s - 1, hh, 0:8, :] = total
        return carry

    lane1 = lax.broadcasted_iota(jnp.int32, (1, LANES), 1)

    lane_p = lax.broadcasted_iota(jnp.int32, (PITCH, LANES), 1)
    edge3 = lax.broadcasted_iota(jnp.int32, (16, LANES), 0) == 0
    lane_half = lax.rem(lane_p, LANES // 2)
    nk = (nd + 4) // COLS
    gm = group_matrix()

    def cost_row(hh, carry):
        for r in range(COLS):
            keep = lane1 < LANES - C * r

            def moved(x, y):
                if r == 0:
                    return x
                s = LANES - C * r
                return jnp.where(keep, pltpu.roll(x, s, 1), pltpu.roll(y, s, 1))

            vt[r] = moved(vt0[hh, 0:40, :], vt0[hh, 1:41, :])
            for side in range(2):
                vte[r, side] = moved(vte0[side, hh, 0:8, :], vte0[side, hh, 1:9, :])
        ref_rows = refx[hh]
        at = pl.multiple_of(hh * PITCH, 16)
        for k in range(nk):
            parts = []
            for r in range(COLS):
                own = vt[r, k : k + WROWS, :]
                side = jnp.where(edge3, vte[r, 1, k : k + 1, :], vte[r, 0, k : k + 1, :])
                prod = ref_rows * jnp.concatenate([own, side], axis=0)
                top = prod.astype(jnp.bfloat16)
                low = (prod - top.astype(jnp.float32)).astype(jnp.bfloat16)
                parts.append(jnp.concatenate([top, low], axis=1))
            cost = jnp.dot(jnp.concatenate(parts, axis=0), gm, preferred_element_type=jnp.float32)
            for r in range(COLS):
                c = cost[r * PITCH : (r + 1) * PITCH]
                x = jnp.where(
                    lane_half < COLS * G,
                    c,
                    jnp.where(lane_half < (COLS + 1) * G, pltpu.roll(c, 1, 0), pltpu.roll(c, PITCH - 1, 0)),
                )
                dd = k * COLS + r
                if dd < 2 or dd >= nd + 2:
                    disp = d0 - 2 + dd
                    x = jnp.where((disp >= 0) & (disp < NDISP), x, 0.0)
                both = jnp.where(lane_p < LANES // 2, xprev[dd], x)
                x1[dd, pl.ds(at, PITCH), :] = both.astype(jnp.bfloat16)
                xprev[dd] = x
        return carry

    arrived(0)
    assemble(0, 0)

    def row_fetching(hh, carry):
        arrived(hh + 1)
        fetch(hh + ahead, carry)
        cost_row(hh, carry)
        return assemble(hh + 1, carry)

    def row_only(hh, carry):
        arrived(hh + 1)
        cost_row(hh, carry)
        return assemble(hh + 1, carry)

    lax.fori_loop(0, HX - ahead, row_fetching, 0)
    lax.fori_loop(HX - ahead, HX - 1, row_only, 0)
    cost_row(HX - 1, 0)
    for dd in range(nk * COLS):
        x1[dd, HX * PITCH : (HX + 1) * PITCH, :] = xprev[dd].astype(jnp.bfloat16)

    rows1 = (H + 2) * PITCH
    row_id = lax.broadcasted_iota(jnp.int32, (rows1, LANES), 0)
    hrow = row_id // PITCH
    col = row_id - hrow * PITCH

    def inside(s):
        above = jnp.where(tiles[s][0] >= 0, 1, 0)
        mid = jnp.where(tiles[s][1] >= 0, 1, 0)
        below = jnp.where(tiles[s][2] >= 0, 1, 0)
        return jnp.where(hrow == 0, above, jnp.where(hrow == H + 1, below, mid))

    valid = jnp.where(col < WROWS, inside(0), jnp.where(col == WROWS, inside(2), inside(1)))
    bias1 = jnp.concatenate([b1[...]] * COLS, axis=1)
    bias2 = jnp.concatenate([b2[...]] * COLS, axis=1)
    lane_h = lax.broadcasted_iota(jnp.int32, (PITCH, LANES), 1)

    def layer1(d):
        lhs = jnp.concatenate(
            [x1[d + a, b * PITCH : b * PITCH + rows1, :] for a in range(4) for b in (1, 3)], axis=1
        )
        pair = jnp.dot(lhs, w1[...], preferred_element_type=jnp.float32)
        for j in range(2):
            y = jnp.maximum(pair[:, j * LANES : (j + 1) * LANES] + bias1, 0.0)
            disp = d0 - 1 + d + j
            least = jnp.where((disp >= 0) & (disp < NDISP), 0, 1)
            y = jnp.where(valid > least, y, 0.0)
            for hh in range(H + 2):
                z = y[hh * PITCH : (hh + 1) * PITCH]
                zr = pltpu.roll(z, C, 1)
                extra = jnp.where(lane_h < CH, pltpu.roll(zr, 1, 0), pltpu.roll(zr, PITCH - 1, 0))
                both = jnp.concatenate([z[:WROWS], extra[:WROWS]], axis=1)
                h2[d + j, hh * WROWS : (hh + 1) * WROWS, :] = both.astype(jnp.bfloat16)

    rows2 = H * WROWS

    def slab_out(d):
        return pltpu.make_async_copy(obuf.at[d], out_ref.at[d], sem_o.at[d])

    def layer2(d):
        lhs = jnp.concatenate(
            [h2[d + a, b * WROWS : b * WROWS + rows2, :] for a in range(4) for b in range(3)], axis=1
        )
        pair = jnp.dot(lhs, w2[...], preferred_element_type=jnp.float32)
        for j in range(2):
            y = ybuf.at[j]
            y[...] = pair[:, j * LANES : (j + 1) * LANES] + bias2
            for i in range(WROWS):
                obuf[d + j, :, i * LANES : (i + 1) * LANES] = y[pl.ds(i, H, stride=WROWS), :]
            slab_out(d + j).start()

    for copy in weights:
        copy.wait()
    layer1(0)
    layer1(2)

    def both_layers(i, carry):
        layer2(2 * i)
        layer1(2 * i + 4)
        return carry

    lax.fori_loop(0, nd // 2 - 1, both_layers, 0)
    layer2(nd - 2)

    def slab_done(d, carry):
        slab_out(d).wait()
        return carry

    lax.fori_loop(0, nd, slab_done, 0)


def group_matrix():
    row = lax.broadcasted_iota(jnp.int32, (2 * LANES, LANES), 0)
    lane = lax.broadcasted_iota(jnp.int32, (2 * LANES, LANES), 1)
    source = lax.rem(row, LANES) // (C // G)
    lane = lax.rem(lane, LANES // 2)
    own = COLS * G
    target = jnp.where(
        lane < own, lane, jnp.where(lane < own + G, lane - G, jnp.where(lane < own + 2 * G, lane - own - G, -1))
    )
    return jnp.where(source == target, 1.0 / (NPV * (C // G)), 0.0).astype(jnp.bfloat16)


def on_device(
    ref_features, partner_lines, line_owner, line_index, line_offset, neighbours,
    conv1_weight, conv1_bias, conv2_weight, conv2_bias,
):
    n_tiles = lax.axis_size("tiles")
    views = lax.axis_size("views")
    nd = NDISP // views
    body = NPV * H * LROWS + H * WROWS
    total = -(-body // (16 * views)) * 16 * views
    vmem = pl.BlockSpec(memory_space=pltpu.VMEM)
    smem = pl.BlockSpec(memory_space=pltpu.SMEM)
    hbm = pl.BlockSpec(memory_space=pl.ANY)
    orders = hop_orders(n_tiles, views)
    dma = pltpu.SemaphoreType.DMA
    gathered, table, w1, w2 = pl.pallas_call(
        partial(gather_kernel, n_tiles, views),
        out_shape=[
            jax.ShapeDtypeStruct((n_tiles, total, LANES), jnp.bfloat16),
            jax.ShapeDtypeStruct((n_tiles, 8, LANES), jnp.int32),
            jax.ShapeDtypeStruct((6 * LANES, LANES), jnp.bfloat16),
            jax.ShapeDtypeStruct((18 * LANES, LANES), jnp.bfloat16),
        ],
        in_specs=[vmem] * 7,
        out_specs=[hbm, hbm, vmem, vmem],
        scratch_shapes=[
            pltpu.VMEM((total, LANES), jnp.float32),
            pltpu.VMEM((total, LANES), jnp.bfloat16),
            pltpu.VMEM((8, LANES), jnp.int32),
            dma((2,)),
            *[dma((1 << len(order),)) for order in orders for _ in range(2)],
        ],
        compiler_params=pltpu.CompilerParams(
            collective_id=0, has_side_effects=True, vmem_limit_bytes=60 << 20
        ),
        name="gather",
    )(
        partner_lines[0].reshape(NPV * H, SW * C),
        ref_features[0],
        line_owner.reshape(1, NPV * H),
        line_index,
        line_offset,
        conv1_weight.reshape(27 * G, CH),
        conv2_weight.reshape(27 * CH, CH),
    )
    nk = (nd + 4) // COLS
    f32, bf16 = jnp.float32, jnp.bfloat16
    out = pl.pallas_call(
        partial(main_kernel, nd),
        out_shape=jax.ShapeDtypeStruct((nd, H, W * CH), f32),
        in_specs=[smem, hbm, hbm, hbm, vmem, hbm, vmem],
        out_specs=hbm,
        scratch_shapes=[
            pltpu.VMEM((8 * LANES, 2 * LANES), bf16),
            pltpu.VMEM((24 * LANES, 2 * LANES), bf16),
            pltpu.VMEM((nd, H, W * CH), f32),
            pltpu.SMEM((n_tiles, 8, LANES), jnp.int32),
            pltpu.VMEM((HX, 3 * NPV, LROWS, LANES), bf16),
            pltpu.VMEM((3, HX * WROWS, LANES), bf16),
            pltpu.VMEM((3 * NPV, LPAD, LANES), f32),
            pltpu.VMEM((HX, 48, LANES), f32),
            pltpu.VMEM((2, HX, 16, LANES), f32),
            pltpu.VMEM((COLS, 40, LANES), f32),
            pltpu.VMEM((COLS, 2, 8, LANES), f32),
            pltpu.VMEM((HX, PITCH, LANES), f32),
            pltpu.VMEM((nk * COLS, PITCH, LANES), f32),
            pltpu.VMEM((nk * COLS, (HX + 1) * PITCH, LANES), bf16),
            pltpu.VMEM((nd + 2, (H + 2) * WROWS, 2 * LANES), bf16),
            pltpu.VMEM((2, H * WROWS, LANES), f32),
            dma((HX,)),
            dma((9,)),
            dma,
            dma((4,)),
            dma((nd,)),
        ],
        compiler_params=pltpu.CompilerParams(vmem_limit_bytes=60 << 20),
        name="volume",
    )(
        neighbours.T,
        table,
        gathered,
        w1,
        conv1_bias[None],
        w2,
        conv2_bias[None],
    )
    return out[None]


def solution(mesh):
    return jax.shard_map(
        on_device,
        mesh=mesh,
        in_specs=(
            P("tiles", None, None),
            P("tiles", None, None, None),
            P("tiles", None, None),
            P("tiles", None),
            P("tiles", None),
            P(),
            P(),
            P(),
            P(),
            P(),
        ),
        out_specs=P("tiles", "views", None, None),
        check_vma=False,
    )
```
